32 devices in a mesh: parts: 2 (over y), gx: 4 (over z), gy: 4 (over x, core).
Axes of the slice: x: 2, y: 2, z: 4, core: 2. Of those that a mesh axis runs over, the one named last changes fastest.
Arguments:
- base_cond: float32 [3, 4, 32, 512], P(None, None, 'gx', 'gy'), may hold values from 0.5 to 2
- base_mass: float32 [4, 32, 512], P(None, 'gx', 'gy'), may hold values from 0.05 to 0.5
- fine_residual: float32 [8, 32, 512], P('parts', 'gx', 'gy'), parts along dimension 0, may hold values from -6 to 6
- point_index: int32 [2], P('parts'), parts along dimension 0, may hold values from 0 to 1048575
- gen_vector: int32 [32], replicated, may hold values from 1 to 1048575
- z_offset: int32 [1], replicated, may hold values from 0 to 508
Outputs:
- coarse_stencil: float32 [27, 4, 16, 256], P(None, 'parts', 'gx', 'gy'), parts along dimension 1
- coarse_solution: float32 [4, 16, 256], P('parts', 'gx', 'gy'), parts along dimension 0
The draws below stay inside these ranges and needn't reach their ends.
There are 2 independent parts, one for each index of `parts`. The reference program is written for one: setup_inputs(seed, part) draws one part's arguments, and reference() takes and returns one part's arrays. A program takes and returns all parts, laid end to end along the dimension named above; an argument that names none is the same for every part. Nothing has to cross between parts.
All inputs are finite; a program needn't handle non-finite values.
Results may differ from the reference program's by a relative error of at most 0.0003.
Values sent between devices are 32-bit elements; how exact they have to be, the bound alone decides.
A program may use at most 128 MiB of HBM per device.

```python
import math
import jax
import jax.numpy as jnp
from jax import lax

FZ = 4
NZG = 512
MODES = 32
QMCN = 1048576
SWEEPS = 4
NX = 32
NY = 512
CZ = 2
CNX = 16
CNY = 256


def set_ends(result, key, low, top_value):
    shape = result.shape
    index_at = [jax.random.randint(jax.random.fold_in(key, axis), (), 0, shape[axis]) for axis in range(len(shape))]
    result = result.at[tuple(index_at)].set(low)
    longest = shape.index(max(shape))
    index_at[longest] = (index_at[longest] + 1) % shape[longest]
    return result.at[tuple(index_at)].set(top_value)


def shard_levels(own_key, extent, split, smallest, largest):
    def one(position, shards_of):
        draws = jax.random.uniform(jax.random.fold_in(jax.random.fold_in(own_key, 6), position), (shards_of,), jnp.float32, smallest / len(split), largest / len(split))
        return jnp.repeat(jnp.exp(draws), extent[position] // shards_of).reshape((-1,) + (1,) * (len(extent) - position - 1))

    gain = one(*split[0])
    for cut in split[1:]:
        gain = gain * one(*cut)
    return gain


def normal_values(rng, extent, scale, reach, cuts=(), kind=jnp.bfloat16):
    values = jax.random.normal(rng, extent, jnp.float32) * scale
    if len(cuts) > 0:
        values = shard_levels(rng, extent, cuts, -0.22, 0.18) * values
    return jnp.clip(values, min=-reach, max=reach).astype(kind)


def setup_inputs(seed: int = 0, part: int = 0) -> dict:
    keys = jax.random.split(jax.random.key(seed), 7)
    part_keys = jax.random.split(jax.random.fold_in(keys[6], part), 7)
    return {
        "base_cond": jnp.clip(jnp.exp(math.log(2.0) - 1.3862944 * jax.random.uniform(keys[0], (3, FZ, NX, NY), jnp.float32) ** shard_levels(keys[0], (3, FZ, NX, NY), ((2, 4), (3, 4)), -0.2, 0.2)), 0.5, 2.0),
        "base_mass": jnp.clip(jnp.exp(math.log(0.5) - 2.3025851 * jax.random.uniform(keys[1], (FZ, NX, NY), jnp.float32) ** shard_levels(keys[1], (FZ, NX, NY), ((1, 4), (2, 4)), -0.2, 0.2)), 0.05, 0.5),
        "fine_residual": normal_values(part_keys[2], (FZ, NX, NY), 1.0, 6.0, ((1, 4), (2, 4)), jnp.float32),
        "point_index": jax.random.randint(part_keys[3], (1,), 0, QMCN).astype(jnp.int32),
        "gen_vector": set_ends(jax.random.randint(keys[4], (MODES,), 1, QMCN), jax.random.fold_in(keys[4], 1), 1, QMCN - 1).astype(jnp.int32),
        "z_offset": jax.random.randint(keys[5], (1,), 0, NZG - FZ + 1).astype(jnp.int32),
    }


omega_value = 0.6


def lattice_shift(point_index, gen_vector):
    product = point_index[0] * gen_vector
    return jnp.remainder(product, QMCN).astype(jnp.float32) / QMCN - 0.5


def field_log(qmc_shift, x_glob, y_glob, z_glob, nx_total, ny_total):
    x_angle = (x_glob.astype(jnp.float32) + 0.5) * (math.pi / nx_total)
    y_angle = (y_glob.astype(jnp.float32) + 0.5) * (math.pi / ny_total)
    z_angle = (z_glob.astype(jnp.float32) + 0.5) * (math.pi / NZG)
    summed = jnp.zeros((z_glob.shape[0], x_glob.shape[0], y_glob.shape[0]), jnp.float32)
    for mode_index in range(qmc_shift.shape[0]):
        amplitude = 1.2 / (1.0 + 0.5 * mode_index)
        angle_sum = (z_angle * (mode_index % 5))[:, None, None] + (x_angle * (1 + mode_index % 4))[None, :, None]
        angle_sum = angle_sum + (y_angle * (1 + (mode_index // 4) % 4))[None, None, :] + 0.7 * mode_index
        summed = summed + (qmc_shift[mode_index] * amplitude) * jnp.cos(angle_sum)
    return summed


def effective(base_cond, base_mass, qmc_shift, x_glob, y_glob, z_local, z_base, nx_total, ny_total):
    z_glob = z_local + z_base
    log_here = field_log(qmc_shift, x_glob, y_glob, z_glob, nx_total, ny_total)
    log_east = field_log(qmc_shift, x_glob + 1, y_glob, z_glob, nx_total, ny_total)
    log_north = field_log(qmc_shift, x_glob, y_glob + 1, z_glob, nx_total, ny_total)
    log_upper = field_log(qmc_shift, x_glob, y_glob, z_glob + 1, nx_total, ny_total)
    open_x = (x_glob + 1 < nx_total)[None, :, None]
    open_y = (y_glob + 1 < ny_total)[None, None, :]
    open_z = (z_local + 1 < z_local.shape[0])[:, None, None]
    cond_x = jnp.where(open_x, base_cond[0] * jnp.exp(0.5 * (log_here + log_east)), 0.0)
    cond_y = jnp.where(open_y, base_cond[1] * jnp.exp(0.5 * (log_here + log_north)), 0.0)
    cond_z = jnp.where(open_z, base_cond[2] * jnp.exp(0.5 * (log_here + log_upper)), 0.0)
    mass_term = base_mass * jnp.exp(log_here)
    return jnp.stack([cond_x, cond_y, cond_z, mass_term]).astype(jnp.float32)


def pad_plane(values):
    return jnp.pad(values, [(0, 0)] * (values.ndim - 2) + [(1, 1), (1, 1)])


def couple(padded, cond_wide):
    cond_east = cond_wide[0, :, 1:-1, 1:-1]
    cond_west = cond_wide[0, :, :-2, 1:-1]
    cond_north = cond_wide[1, :, 1:-1, 1:-1]
    cond_south = cond_wide[1, :, 1:-1, :-2]
    cond_upper = cond_wide[2, :, 1:-1, 1:-1]
    cond_lower = jnp.pad(cond_upper, ((1, 0), (0, 0), (0, 0)))[:-1]
    middle = padded[..., 1:-1, 1:-1]
    lead = [(0, 0)] * (middle.ndim - 3)
    below = jnp.pad(middle, lead + [(1, 0), (0, 0), (0, 0)])[..., :-1, :, :]
    above = jnp.pad(middle, lead + [(0, 1), (0, 0), (0, 0)])[..., 1:, :, :]
    summed = cond_west * padded[..., :-2, 1:-1] + cond_east * padded[..., 2:, 1:-1]
    summed = summed + cond_south * padded[..., 1:-1, :-2] + cond_north * padded[..., 1:-1, 2:]
    return summed + cond_lower * below + cond_upper * above


def weights(cond_wide, x_glob, y_glob, z_local, nx_total, ny_total):
    cond_east = cond_wide[0, :, 1:-1, 1:-1]
    cond_west = cond_wide[0, :, :-2, 1:-1]
    cond_north = cond_wide[1, :, 1:-1, 1:-1]
    cond_south = cond_wide[1, :, 1:-1, :-2]
    cond_upper = cond_wide[2, :, 1:-1, 1:-1]
    cond_lower = jnp.pad(cond_upper, ((1, 0), (0, 0), (0, 0)))[:-1]
    mass_term = cond_wide[3, :, 1:-1, 1:-1]
    odd_x = (x_glob % 2 == 1)[None, :, None]
    odd_y = (y_glob % 2 == 1)[None, None, :]
    odd_z = (z_local % 2 == 1)[:, None, None]
    inside = ((x_glob >= 0) & (x_glob < nx_total))[None, :, None] & ((y_glob >= 0) & (y_glob < ny_total))[None, None, :]
    pair_x = cond_east + cond_west
    pair_y = cond_north + cond_south
    pair_z = cond_upper + cond_lower
    denominator = mass_term + jnp.where(odd_x, pair_x, 0.0) + jnp.where(odd_y, pair_y, 0.0) + jnp.where(odd_z, pair_z, 0.0)
    reciprocal = jnp.where(inside, 1.0 / jnp.where(inside, denominator, 1.0), 0.0)
    odd_count = odd_x.astype(jnp.int32) + odd_y.astype(jnp.int32) + odd_z.astype(jnp.int32)
    weight_one = jnp.where(odd_count == 1, reciprocal, 0.0)
    weight_two = jnp.where(odd_count == 2, reciprocal, 0.0)
    weight_three = jnp.where(odd_count == 3, reciprocal, 0.0)
    diagonal = mass_term + pair_x + pair_y + pair_z
    return weight_one, weight_two, weight_three, diagonal


def prolong_apply(seed_wide, cond_wide, weight_one, weight_two, weight_three, diagonal, spread):
    level_zero = seed_wide[..., 1:-1, 1:-1]
    level_one = level_zero + weight_one * couple(seed_wide, cond_wide)
    level_two = level_one + weight_two * couple(spread(level_one), cond_wide)
    level_three = level_two + weight_three * couple(spread(level_two), cond_wide)
    return diagonal * level_three - couple(spread(level_three), cond_wide)


def restrict(applied, cond_wide, weight_one, weight_two, weight_three, spread):
    applied = applied + couple(spread(weight_three * applied), cond_wide)
    applied = applied + couple(spread(weight_two * applied), cond_wide)
    return applied + couple(spread(weight_one * applied), cond_wide)


def colour_table(coords, upper_limit):
    usable = (coords % 2 == 0) & (coords >= 0) & (coords < upper_limit)
    colour_of = (coords // 2) % 3
    return jnp.stack([jnp.where(usable & (colour_of == colour), 1.0, 0.0) for colour in range(3)]).astype(jnp.float32)


def offset_table(coords):
    return jnp.stack([jnp.stack([jnp.where((coords + offset - 1) % 3 == colour, 1.0, 0.0) for colour in range(3)]) for offset in range(3)]).astype(jnp.float32)


def select_offsets(probes, q_z, q_x, q_y):
    table_z = offset_table(q_z)
    table_x = offset_table(q_x)
    table_y = offset_table(q_y)
    plane_count, size_x, size_y = probes.shape[1:]
    grouped = probes.reshape(3, 3, 3, plane_count, size_x, size_y)
    section_one = jnp.sum(table_z[:, :, None, None, :, None, None] * grouped[None], axis=1)
    section_two = jnp.sum(table_x[None, :, :, None, None, :, None] * section_one[:, None], axis=2)
    section_three = jnp.sum(table_y[None, None, :, :, None, None, :] * section_two[:, :, None], axis=3)
    return section_three.reshape(27, plane_count, size_x, size_y)


def apply_coarse(stencil, padded):
    plane_count, size_x, size_y = stencil.shape[1:]
    deep_pad = jnp.pad(padded, ((1, 1), (0, 0), (0, 0)))
    summed = jnp.zeros((plane_count, size_x, size_y), jnp.float32)
    for offset_z in range(3):
        for offset_x in range(3):
            for offset_y in range(3):
                summed = summed + stencil[9 * offset_z + 3 * offset_x + offset_y] * deep_pad[offset_z:offset_z + plane_count, offset_x:offset_x + size_x, offset_y:offset_y + size_y]
    return summed


def jacobi(stencil, coarse_rhs, diag_safe, spread):
    solution = omega_value * coarse_rhs / diag_safe
    for sweep_index in range(SWEEPS - 1):
        solution = solution + omega_value * (coarse_rhs - apply_coarse(stencil, spread(solution))) / diag_safe
    return solution


def reference(base_cond, base_mass, fine_residual, point_index, gen_vector, z_offset):
    qmc_shift = lattice_shift(point_index, gen_vector)
    x_glob = jnp.arange(NX, dtype=jnp.int32)
    y_glob = jnp.arange(NY, dtype=jnp.int32)
    z_local = jnp.arange(FZ, dtype=jnp.int32)
    coeffs = effective(base_cond, base_mass, qmc_shift, x_glob, y_glob, z_local, z_offset[0], NX, NY)
    cond_wide = pad_plane(coeffs)
    weight_one, weight_two, weight_three, diagonal = weights(cond_wide, x_glob, y_glob, z_local, NX, NY)
    table_z = colour_table(z_local, FZ)
    table_x = colour_table(jnp.arange(-1, NX + 1, dtype=jnp.int32), NX)
    table_y = colour_table(jnp.arange(-1, NY + 1, dtype=jnp.int32), NY)

    def one_probe(colour_index):
        seed_wide = table_z[colour_index // 9][:, None, None] * table_x[(colour_index // 3) % 3][None, :, None] * table_y[colour_index % 3][None, None, :]
        applied = prolong_apply(seed_wide, cond_wide, weight_one, weight_two, weight_three, diagonal, pad_plane)
        restricted = restrict(applied, cond_wide, weight_one, weight_two, weight_three, pad_plane)
        return restricted[::2, ::2, ::2]

    probes = lax.map(one_probe, jnp.arange(27, dtype=jnp.int32))
    coarse_rhs = restrict(fine_residual, cond_wide, weight_one, weight_two, weight_three, pad_plane)[::2, ::2, ::2]
    stencil = select_offsets(probes, jnp.arange(CZ, dtype=jnp.int32), jnp.arange(CNX, dtype=jnp.int32), jnp.arange(CNY, dtype=jnp.int32))
    solution = jacobi(stencil, coarse_rhs, stencil[13], pad_plane)
    return stencil, solution
```

```python
import functools
import itertools
import math

import jax
import jax.numpy as jnp
from jax import lax
from jax.experimental import pallas as pl
from jax.experimental.pallas import tpu as pltpu
from jax.sharding import PartitionSpec as P

MESH = pl.DeviceIdType.MESH
NZG = 512
QMCN = 1048576
SWEEPS = 4
OMEGA = 0.6
MODES = 32
HALO = 4
CLASSES = list(itertools.product((0, 1), repeat=3))
FIELDS = 5
AXIS_FIELD = (2, 0, 1)
DIRECTIONS = [(sx, sy) for sx in (-1, 0, 1) for sy in (-1, 0, 1) if (sx, sy) != (0, 0)]
ROWS = 24
LANES = 128


def cos_turns(turns):
    rest = 0.25 - jnp.abs(turns - jnp.round(turns))
    angle = rest * (2.0 * math.pi)
    square = angle * angle
    series = 1.0 / 6227020800.0
    for term in (-1.0 / 39916800.0, 1.0 / 362880.0, -1.0 / 5040.0, 1.0 / 120.0, -1.0 / 6.0, 1.0):
        series = series * square + term
    return series * angle


def shift(value, axis, step):
    if axis == 2:
        return pltpu.roll(value, (-step) % LANES, 1)
    return pltpu.roll(value, (-step * (1, 2)[axis]) % ROWS, 0)


def lanes_of(value, index):
    return jnp.take_along_axis(value, index, axis=1, mode="promise_in_bounds")


def flip(cls, axis):
    return tuple(1 - p if a == axis else p for a, p in enumerate(cls))


def split_lanes(tile, index):
    return lanes_of(tile, index)


def field_roots(point_ref, gen_ref, zoff_ref, x_first, y_first, nx_total, ny_total):
    point = point_ref[0]
    lane = lax.broadcasted_iota(jnp.int32, (1, 2 * MODES), 1)
    mode = jnp.where(lane < MODES, lane, lane - MODES)
    shifts = jnp.zeros((1, 2 * MODES), jnp.int32)
    for k in range(MODES):
        shifts = jnp.where(mode == k, (point * gen_ref[k]) & (QMCN - 1), shifts)
    modef = mode.astype(jnp.float32)
    amplitude = (shifts.astype(jnp.float32) / QMCN - 0.5) * (1.2 / (1.0 + 0.5 * modef))
    freq_z = modef - 5.0 * jnp.floor((modef + 0.5) * 0.2)
    freq_x = (1 + (mode & 3)).astype(jnp.float32)
    phase = modef * (0.7 / (2.0 * math.pi)) - jnp.where(lane < MODES, 0.0, 0.25)
    row = lax.broadcasted_iota(jnp.int32, (ROWS, 1), 0)
    z_row = (zoff_ref[0] + 2 * (row & 1)).astype(jnp.float32) + 0.5
    x_row = (x_first + 2 * ((row >> 1) - HALO)).astype(jnp.float32) + 0.5
    left = []
    for pz, px in itertools.product((0, 1), repeat=2):
        turns = (z_row + pz) * (freq_z / (2.0 * NZG)) + (x_row + px) * (freq_x / (2.0 * nx_total))
        left.append(amplitude * cos_turns(turns + phase))
    left = jnp.concatenate(left, axis=0)
    mode_row = lax.broadcasted_iota(jnp.int32, (2 * MODES, 1), 0)
    freq_y = (1 + ((mode_row >> 2) & 3)).astype(jnp.float32)
    quarter = jnp.where(mode_row < MODES, 0.0, 0.25)
    place = lax.broadcasted_iota(jnp.int32, (1, LANES), 1)
    coarse = jnp.where(place < LANES // 2 + HALO, place, place - LANES)
    right = []
    for py in (0, 1):
        y_place = (y_first + 2 * coarse + py).astype(jnp.float32) + 0.5
        right.append(cos_turns(freq_y * (y_place / (2.0 * ny_total)) + quarter))
    right = jnp.concatenate(right, axis=1)
    logs = jnp.dot(left, right, precision=lax.Precision.HIGHEST, preferred_element_type=jnp.float32)
    roots = jnp.exp(0.5 * logs)
    out = {}
    for n, (pz, px) in enumerate(itertools.product((0, 1), repeat=2)):
        for py in (0, 1):
            out[pz, px, py] = roots[n * ROWS:(n + 1) * ROWS, py * LANES:(py + 1) * LANES]
    return out


def coefficients(base, roots, x_first, y_first, nx_total, ny_total):
    row = lax.broadcasted_iota(jnp.int32, (ROWS, LANES), 0)
    place = lax.broadcasted_iota(jnp.int32, (ROWS, LANES), 1)
    x_even = x_first + 2 * ((row >> 1) - HALO)
    half = LANES // 2
    y_even = y_first + 2 * jnp.where(place < half + HALO, place, place - LANES)
    inside = (x_even >= 0) & (x_even < nx_total) & (y_even >= 0) & (y_even < ny_total)
    inside = inside & ((place < half + HALO) | (place >= LANES - HALO))
    closed = (
        inside & ((row & 1) == 0),
        inside & (x_even + 2 < nx_total),
        inside & (y_even + 2 < ny_total),
    )
    cond, mass, residual = {}, {}, {}
    for cls in CLASSES:
        for axis in range(3):
            other = roots[flip(cls, axis)]
            if cls[axis]:
                other = shift(other, axis, 1)
            value = base(AXIS_FIELD[axis], cls) * roots[cls] * other
            cond[axis, cls] = jnp.where(closed[axis] if cls[axis] else inside, value, 0.0)
        mass[cls] = jnp.where(inside, base(3, cls) * (roots[cls] * roots[cls]), 1.0)
        residual[cls] = jnp.where(inside, base(4, cls), 0.0)
    return cond, mass, residual


def galerkin(cond, mass, residual):
    low = {}
    for cls in CLASSES:
        for axis in range(3):
            own = cond[axis, flip(cls, axis)]
            low[axis, cls] = own if cls[axis] else shift(own, axis, -1)

    weight = {((0, 0, 0), (0, 0, 0)): None}
    for cls in sorted(CLASSES, key=sum)[1:]:
        odd = [a for a in range(3) if cls[a]]
        total = mass[cls]
        for a in odd:
            total = total + (low[a, cls] + cond[a, cls])
        recip = 1.0 / total
        for corner in itertools.product(*[(0, 1) if p else (0,) for p in cls]):
            summed = None
            for a in odd:
                face = cond[a, cls] if corner[a] else low[a, cls]
                part = weight[flip(cls, a), tuple(0 if b == a else s for b, s in enumerate(corner))]
                if part is None:
                    term = face
                else:
                    term = face * (shift(part, a, 1) if corner[a] else part)
                summed = term if summed is None else summed + term
            weight[cls, corner] = recip * summed

    def wanted(offset):
        return offset >= (0, 0, 0)

    parts = {}

    def add(corner, offset, value):
        slot = parts.setdefault(offset, {})
        slot[corner] = slot[corner] + value if corner in slot else value

    for cls in sorted(CLASSES, key=sum)[:-1]:
        even = [a for a in range(3) if not cls[a]]
        pairs = None
        for a in even:
            pair = low[a, cls] + cond[a, cls]
            pairs = pair if pairs is None else pairs + pair
        if sum(cls) == 0:
            pairs = pairs + mass[cls]
        corners = list(itertools.product(*[(0, 1) if p else (0,) for p in cls]))
        applied = {}
        for corner in corners:
            own = weight[cls, corner]
            centre = pairs if own is None else pairs * own
            for a in even:
                up = flip(cls, a)
                high = tuple(1 if b == a else s for b, s in enumerate(corner))
                to_low = cond[a, up] * weight[up, corner]
                to_high = cond[a, up] * weight[up, high]
                centre = centre - shift(to_high, a, -1) - cond[a, cls] * weight[up, corner]
                below = tuple(-1 if b == a else s for b, s in enumerate(corner))
                applied[below] = -shift(to_low, a, -1)
                applied[high] = -(cond[a, cls] * weight[up, high])
            applied[corner] = centre
        for corner in corners:
            own = weight[cls, corner]
            for target, value in applied.items():
                offset = tuple(t - s for t, s in zip(target, corner))
                if wanted(offset):
                    add(corner, offset, value if own is None else own * value)

    def collect(slot):
        for axis in range(3):
            merged = {}
            for corner, value in slot.items():
                if corner[axis] == 0:
                    merged[corner] = merged[corner] + value if corner in merged else value
            for corner, value in slot.items():
                if corner[axis] == 1:
                    key = tuple(0 if b == axis else s for b, s in enumerate(corner))
                    moved = shift(value, axis, -1)
                    merged[key] = merged[key] + moved if key in merged else moved
            slot = merged
        return slot[0, 0, 0]

    stencil = {offset: collect(slot) for offset, slot in parts.items()}
    for offset in list(stencil):
        if offset != (0, 0, 0):
            value = stencil[offset]
            for axis, step in enumerate(offset):
                if step:
                    value = shift(value, axis, -step)
            stencil[tuple(-o for o in offset)] = value

    slot = {(0, 0, 0): residual[0, 0, 0]}
    for (cls, corner), own in weight.items():
        if own is not None:
            term = own * residual[cls]
            slot[corner] = slot[corner] + term if corner in slot else term
    return stencil, collect(slot)


def sweep_all(stencil, rhs):
    row = lax.broadcasted_iota(jnp.int32, (ROWS, LANES), 0)
    place = lax.broadcasted_iota(jnp.int32, (ROWS, LANES), 1)
    reach = HALO - 1
    valid = (row >= 2) & (row < ROWS - 2)
    valid = valid & ((place < LANES // 2 + reach) | (place >= LANES - reach))
    scale = jnp.where(valid, OMEGA / jnp.where(valid, stencil[0, 0, 0], 1.0), 0.0)
    values = rhs * scale
    for _ in range(SWEEPS - 1):
        rest = rhs
        for dz in (-1, 0, 1):
            in_z = shift(values, 0, dz) if dz else values
            for dx in (-1, 0, 1):
                in_x = shift(in_z, 1, dx) if dx else in_z
                for dy in (-1, 0, 1):
                    in_y = shift(in_x, 2, dy) if dy else in_x
                    rest = rest - stencil[dz, dx, dy] * in_y
        values = values + rest * scale
    return values


def kernel(
    counts, cond_hbm, mass_hbm, res_hbm, point_ref, gen_ref, zoff_ref, stencil_ref, solution_ref,
    cond_in, mass_in, res_in, own, strip, side, strips, wide, rows_out,
    in_sem, send_sem, recv_sem,
):
    parts_at = lax.axis_index("parts")
    gx, gy = lax.axis_index("gx"), lax.axis_index("gy")
    nx_devices, ny_devices = counts
    width_x, width_y = mass_in.shape[1:]
    x_first, y_first = gx * width_x, gy * width_y
    nx_total, ny_total = nx_devices * width_x, ny_devices * width_y

    def present(sx, sy):
        conditions = []
        if sx:
            conditions.append(gx > 0 if sx < 0 else gx < nx_devices - 1)
        if sy:
            conditions.append(gy > 0 if sy < 0 else gy < ny_devices - 1)
        return functools.reduce(jnp.logical_and, conditions)

    barrier = pltpu.get_barrier_semaphore()
    neighbours = 0
    for sx, sy in DIRECTIONS:
        there = present(sx, sy)
        neighbours = neighbours + there.astype(jnp.int32)

        @pl.when(there)
        def _():
            pl.semaphore_signal(
                barrier, inc=1, device_id=(parts_at, gx + sx, gy + sy), device_id_type=MESH
            )

    loads = [
        pltpu.make_async_copy(source, target, in_sem.at[n])
        for n, (source, target) in enumerate(
            ((cond_hbm, cond_in), (mass_hbm, mass_in), (res_hbm, res_in))
        )
    ]
    for load in loads:
        load.start()
    for load in loads:
        load.wait()

    lane = lax.broadcasted_iota(jnp.int32, (8, LANES), 1)
    half = LANES // 2
    to_halves = jnp.where(lane < half, 2 * lane, 2 * lane - (LANES - 1))
    step = lane & 15
    to_strip = step + jnp.where(
        step < 4, half - 4, jnp.where(step < 8, LANES - 8, jnp.where(step < 12, -8, half - 12))
    )
    packs = [None] * 3
    for field in range(FIELDS):
        for pz in (0, 1):
            for px in (0, 1):
                t = 4 * field + 2 * pz + px
                for zc in (0, 1):
                    plane = 2 * zc + pz
                    if field < 3:
                        piece = cond_in[field, plane, pl.ds(px, 4, stride=2), :]
                    else:
                        source = mass_in if field == 3 else res_in
                        piece = source[plane, pl.ds(px, 4, stride=2), :]
                    own[t, pl.ds(zc, 4, stride=2), :] = piece
                halves = lanes_of(own[t], to_halves)
                own[t] = halves
                packed = lanes_of(halves, to_strip)
                word, group = divmod(t, 8)
                if packs[word] is None:
                    packs[word] = packed
                else:
                    packs[word] = jnp.where((lane >> 4) == group, packed, packs[word])
    for word in range(3):
        strip[word] = packs[word]

    pl.semaphore_wait(barrier, neighbours)

    def copy_to(n):
        sx, sy = DIRECTIONS[n]
        if sy == 0:
            source, target = own, side.at[0 if sx == 1 else 1]
        else:
            source, target = strip, strips.at[n]
        return pltpu.make_async_remote_copy(
            src_ref=source,
            dst_ref=target,
            send_sem=send_sem.at[n],
            recv_sem=recv_sem.at[n],
            device_id=(parts_at, gx + sx, gy + sy),
            device_id_type=MESH,
        )

    for n, (sx, sy) in enumerate(DIRECTIONS):
        @pl.when(present(sx, sy))
        def _():
            copy_to(n).start()

    roots = field_roots(point_ref, gen_ref, zoff_ref, x_first, y_first, nx_total, ny_total)

    for n, (sx, sy) in enumerate(DIRECTIONS):
        @pl.when(present(-sx, -sy))
        def _():
            copy_to(n).wait_recv()

        @pl.when(present(sx, sy))
        def _():
            copy_to(n).wait_send()

    merged = []
    for from_x in (-1, 0, 1):
        from_low = strips.at[DIRECTIONS.index((-from_x, 1))]
        from_high = strips.at[DIRECTIONS.index((-from_x, -1))]
        merged.append([jnp.where(step < 8, from_low[w], from_high[w]) for w in range(3)])
    for t in range(4 * FIELDS):
        word, group = divmod(t, 8)
        for block in range(3):
            tile = (side.at[0], own, side.at[1])[block][t]
            strip_tile = merged[block][word]
            for py in (0, 1):
                index = 16 * group + 4 * py + jnp.where(lane < half + 8, lane - half + 8, lane - (LANES - 4))
                index = jnp.where((lane >= half) & ((lane < half + 4) | (lane >= LANES - 4)), index, 0)
                edge = lanes_of(strip_tile, index)
                middle = pltpu.roll(tile, half, 1) if py else tile
                wide[2 * t + py, pl.ds(8 * block, 8), :] = jnp.where(lane < half, middle, edge)

    def base(field, cls):
        return wide[8 * field + 4 * cls[0] + 2 * cls[1] + cls[2]]

    cond, mass, residual = coefficients(base, roots, x_first, y_first, nx_total, ny_total)
    stencil, rhs = galerkin(cond, mass, residual)
    solved = sweep_all(stencil, rhs)
    for (dz, dx, dy), value in stencil.items():
        rows_out[9 * (dz + 1) + 3 * (dx + 1) + (dy + 1)] = value[8:16]
    rows_out[27] = solved[8:16]
    for zc in (0, 1):
        for d in range(27):
            stencil_ref[d, zc] = rows_out[d, pl.ds(zc, 4, stride=2), :][:, :half]
        solution_ref[zc] = rows_out[27, pl.ds(zc, 4, stride=2), :][:, :half]


def solution(mesh):
    counts = (mesh.shape["gx"], mesh.shape["gy"])

    def on_device(base_cond, base_mass, fine_residual, point_index, gen_vector, z_offset):
        planes, width_x, width_y = base_mass.shape
        assert (planes, width_x, width_y) == (4, 8, LANES)
        tiles = 4 * FIELDS
        return pl.pallas_call(
            functools.partial(kernel, counts),
            out_shape=(
                jax.ShapeDtypeStruct((27, planes // 2, width_x // 2, width_y // 2), jnp.float32),
                jax.ShapeDtypeStruct((planes // 2, width_x // 2, width_y // 2), jnp.float32),
            ),
            in_specs=[pl.BlockSpec(memory_space=pl.ANY)] * 3
            + [pl.BlockSpec(memory_space=pltpu.SMEM)] * 3,
            out_specs=[pl.BlockSpec(memory_space=pltpu.VMEM)] * 2,
            scratch_shapes=[
                pltpu.VMEM((3, planes, width_x, width_y), jnp.float32),
                pltpu.VMEM((planes, width_x, width_y), jnp.float32),
                pltpu.VMEM((planes, width_x, width_y), jnp.float32),
                pltpu.VMEM((tiles, 8, LANES), jnp.float32),
                pltpu.VMEM((3, 8, LANES), jnp.float32),
                pltpu.VMEM((2, tiles, 8, LANES), jnp.float32),
                pltpu.VMEM((8, 3, 8, LANES), jnp.float32),
                pltpu.VMEM((2 * tiles, ROWS, LANES), jnp.float32),
                pltpu.VMEM((28, 8, LANES), jnp.float32),
                pltpu.SemaphoreType.DMA((3,)),
                pltpu.SemaphoreType.DMA((8,)),
                pltpu.SemaphoreType.DMA((8,)),
            ],
            compiler_params=pltpu.CompilerParams(
                collective_id=0, has_side_effects=True, vmem_limit_bytes=32 * 1024 * 1024
            ),
        )(base_cond, base_mass, fine_residual, point_index, gen_vector, z_offset)

    return jax.shard_map(
        on_device,
        mesh=mesh,
        in_specs=(
            P(None, None, "gx", "gy"),
            P(None, "gx", "gy"),
            P("parts", "gx", "gy"),
            P("parts"),
            P(),
            P(),
        ),
        out_specs=(P(None, "parts", "gx", "gy"), P("parts", "gx", "gy")),
        check_vma=False,
    )
```

```python
import functools
import itertools
import math

import jax
import jax.numpy as jnp
from jax import lax
from jax.experimental import pallas as pl
from jax.experimental.pallas import tpu as pltpu
from jax.sharding import PartitionSpec as P

MESH = pl.DeviceIdType.MESH
NZG = 512
QMCN = 1048576
SWEEPS = 4
OMEGA = 0.6
MODES = 32
HALO = 4
CLASSES = list(itertools.product((0, 1), repeat=3))
FIELDS = 5
AXIS_FIELD = (2, 0, 1)
DIRECTIONS = [(sx, sy) for sx in (-1, 0, 1) for sy in (-1, 0, 1) if (sx, sy) != (0, 0)]
ROWS = 24
LANES = 128
VMEM_GRANT = 60 * 1024 * 1024


def cos_turns(turns):
    rest = 0.25 - jnp.abs(turns - jnp.round(turns))
    angle = rest * (2.0 * math.pi)
    square = angle * angle
    series = 1.0 / 6227020800.0
    for term in (-1.0 / 39916800.0, 1.0 / 362880.0, -1.0 / 5040.0, 1.0 / 120.0, -1.0 / 6.0, 1.0):
        series = series * square + term
    return series * angle


def shift(value, axis, step):
    if axis == 2:
        return pltpu.roll(value, (-step) % LANES, 1)
    return pltpu.roll(value, (-step * (1, 2)[axis]) % ROWS, 0)


def lanes_of(value, index):
    return jnp.take_along_axis(value, index, axis=1, mode="promise_in_bounds")


def flip(cls, axis):
    return tuple(1 - p if a == axis else p for a, p in enumerate(cls))


def split_lanes(tile, index):
    return lanes_of(tile, index)


def field_roots(point_ref, gen_ref, zoff_ref, x_first, y_first, nx_total, ny_total):
    point = point_ref[0, 0]
    lane = lax.broadcasted_iota(jnp.int32, (1, 2 * MODES), 1)
    mode = jnp.where(lane < MODES, lane, lane - MODES)
    shifts = jnp.zeros((1, 2 * MODES), jnp.int32)
    for k in range(MODES):
        shifts = jnp.where(mode == k, (point * gen_ref[k]) & (QMCN - 1), shifts)
    modef = mode.astype(jnp.float32)
    amplitude = (shifts.astype(jnp.float32) / QMCN - 0.5) * (1.2 / (1.0 + 0.5 * modef))
    freq_z = modef - 5.0 * jnp.floor((modef + 0.5) * 0.2)
    freq_x = (1 + (mode & 3)).astype(jnp.float32)
    phase = modef * (0.7 / (2.0 * math.pi)) - jnp.where(lane < MODES, 0.0, 0.25)
    row = lax.broadcasted_iota(jnp.int32, (ROWS, 1), 0)
    z_row = (zoff_ref[0, 0] + 2 * (row & 1)).astype(jnp.float32) + 0.5
    x_row = (x_first + 2 * ((row >> 1) - HALO)).astype(jnp.float32) + 0.5
    left = []
    for pz, px in itertools.product((0, 1), repeat=2):
        turns = (z_row + pz) * (freq_z / (2.0 * NZG)) + (x_row + px) * (freq_x / (2.0 * nx_total))
        left.append(amplitude * cos_turns(turns + phase))
    left = jnp.concatenate(left, axis=0)
    mode_row = lax.broadcasted_iota(jnp.int32, (2 * MODES, 1), 0)
    freq_y = (1 + ((mode_row >> 2) & 3)).astype(jnp.float32)
    quarter = jnp.where(mode_row < MODES, 0.0, 0.25)
    place = lax.broadcasted_iota(jnp.int32, (1, LANES), 1)
    coarse = jnp.where(place < LANES // 2 + HALO, place, place - LANES)
    right = []
    for py in (0, 1):
        y_place = (y_first + 2 * coarse + py).astype(jnp.float32) + 0.5
        right.append(cos_turns(freq_y * (y_place / (2.0 * ny_total)) + quarter))
    right = jnp.concatenate(right, axis=1)
    logs = jnp.dot(left, right, precision=lax.Precision.HIGHEST, preferred_element_type=jnp.float32)
    roots = jnp.exp(0.5 * logs)
    out = {}
    for n, (pz, px) in enumerate(itertools.product((0, 1), repeat=2)):
        for py in (0, 1):
            out[pz, px, py] = roots[n * ROWS:(n + 1) * ROWS, py * LANES:(py + 1) * LANES]
    return out


def coefficients(base, roots, x_first, y_first, nx_total, ny_total):
    row = lax.broadcasted_iota(jnp.int32, (ROWS, LANES), 0)
    place = lax.broadcasted_iota(jnp.int32, (ROWS, LANES), 1)
    x_even = x_first + 2 * ((row >> 1) - HALO)
    half = LANES // 2
    y_even = y_first + 2 * jnp.where(place < half + HALO, place, place - LANES)
    inside = (x_even >= 0) & (x_even < nx_total) & (y_even >= 0) & (y_even < ny_total)
    inside = inside & ((place < half + HALO) | (place >= LANES - HALO))
    closed = (
        inside & ((row & 1) == 0),
        inside & (x_even + 2 < nx_total),
        inside & (y_even + 2 < ny_total),
    )
    cond, mass, residual = {}, {}, {}
    for cls in CLASSES:
        for axis in range(3):
            other = roots[flip(cls, axis)]
            if cls[axis]:
                other = shift(other, axis, 1)
            value = base(AXIS_FIELD[axis], cls) * roots[cls] * other
            cond[axis, cls] = jnp.where(closed[axis] if cls[axis] else inside, value, 0.0)
        mass[cls] = jnp.where(inside, base(3, cls) * (roots[cls] * roots[cls]), 1.0)
        residual[cls] = jnp.where(inside, base(4, cls), 0.0)
    return cond, mass, residual


def galerkin(cond, mass, residual):
    low = {}
    for cls in CLASSES:
        for axis in range(3):
            own = cond[axis, flip(cls, axis)]
            low[axis, cls] = own if cls[axis] else shift(own, axis, -1)

    weight = {((0, 0, 0), (0, 0, 0)): None}
    for cls in sorted(CLASSES, key=sum)[1:]:
        odd = [a for a in range(3) if cls[a]]
        total = mass[cls]
        for a in odd:
            total = total + (low[a, cls] + cond[a, cls])
        recip = 1.0 / total
        for corner in itertools.product(*[(0, 1) if p else (0,) for p in cls]):
            summed = None
            for a in odd:
                face = cond[a, cls] if corner[a] else low[a, cls]
                part = weight[flip(cls, a), tuple(0 if b == a else s for b, s in enumerate(corner))]
                if part is None:
                    term = face
                else:
                    term = face * (shift(part, a, 1) if corner[a] else part)
                summed = term if summed is None else summed + term
            weight[cls, corner] = recip * summed

    def wanted(offset):
        return offset >= (0, 0, 0)

    parts = {}

    def add(corner, offset, value):
        slot = parts.setdefault(offset, {})
        slot[corner] = slot[corner] + value if corner in slot else value

    for cls in sorted(CLASSES, key=sum)[:-1]:
        even = [a for a in range(3) if not cls[a]]
        pairs = None
        for a in even:
            pair = low[a, cls] + cond[a, cls]
            pairs = pair if pairs is None else pairs + pair
        if sum(cls) == 0:
            pairs = pairs + mass[cls]
        corners = list(itertools.product(*[(0, 1) if p else (0,) for p in cls]))
        applied = {}
        for corner in corners:
            own = weight[cls, corner]
            centre = pairs if own is None else pairs * own
            for a in even:
                up = flip(cls, a)
                high = tuple(1 if b == a else s for b, s in enumerate(corner))
                to_low = cond[a, up] * weight[up, corner]
                to_high = cond[a, up] * weight[up, high]
                centre = centre - shift(to_high, a, -1) - cond[a, cls] * weight[up, corner]
                below = tuple(-1 if b == a else s for b, s in enumerate(corner))
                applied[below] = -shift(to_low, a, -1)
                applied[high] = -(cond[a, cls] * weight[up, high])
            applied[corner] = centre
        for corner in corners:
            own = weight[cls, corner]
            for target, value in applied.items():
                offset = tuple(t - s for t, s in zip(target, corner))
                if wanted(offset):
                    add(corner, offset, value if own is None else own * value)

    def collect(slot):
        for axis in range(3):
            merged = {}
            for corner, value in slot.items():
                if corner[axis] == 0:
                    merged[corner] = merged[corner] + value if corner in merged else value
            for corner, value in slot.items():
                if corner[axis] == 1:
                    key = tuple(0 if b == axis else s for b, s in enumerate(corner))
                    moved = shift(value, axis, -1)
                    merged[key] = merged[key] + moved if key in merged else moved
            slot = merged
        return slot[0, 0, 0]

    stencil = {offset: collect(slot) for offset, slot in parts.items()}
    for offset in list(stencil):
        if offset != (0, 0, 0):
            value = stencil[offset]
            for axis, step in enumerate(offset):
                if step:
                    value = shift(value, axis, -step)
            stencil[tuple(-o for o in offset)] = value

    slot = {(0, 0, 0): residual[0, 0, 0]}
    for (cls, corner), own in weight.items():
        if own is not None:
            term = own * residual[cls]
            slot[corner] = slot[corner] + term if corner in slot else term
    return stencil, collect(slot)


def sweep_all(stencil, rhs):
    row = lax.broadcasted_iota(jnp.int32, (ROWS, LANES), 0)
    place = lax.broadcasted_iota(jnp.int32, (ROWS, LANES), 1)
    reach = HALO - 1
    valid = (row >= 2) & (row < ROWS - 2)
    valid = valid & ((place < LANES // 2 + reach) | (place >= LANES - reach))
    scale = jnp.where(valid, OMEGA / jnp.where(valid, stencil[0, 0, 0], 1.0), 0.0)
    values = rhs * scale
    for _ in range(SWEEPS - 1):
        rest = rhs
        for dz in (-1, 0, 1):
            in_z = shift(values, 0, dz) if dz else values
            for dx in (-1, 0, 1):
                in_x = shift(in_z, 1, dx) if dx else in_z
                for dy in (-1, 0, 1):
                    in_y = shift(in_x, 2, dy) if dy else in_x
                    rest = rest - stencil[dz, dx, dy] * in_y
        values = values + rest * scale
    return values


def place_of(counts, widths):
    gx, gy = lax.axis_index("gx"), lax.axis_index("gy")
    (nx_devices, ny_devices), (width_x, width_y) = counts, widths
    return gx * width_x, gy * width_y, nx_devices * width_x, ny_devices * width_y


def exchange(
    counts, widths, cond_hbm, mass_hbm, res_hbm, point_hbm, gen_hbm, zoff_hbm,
    own_hbm, side, strips, roots_hbm,
    cond_in, mass_in, res_in, point_ref, gen_ref, zoff_ref, own, strip, roots_out,
    in_sem, send_sem, recv_sem, out_sem,
):
    parts_at = lax.axis_index("parts")
    gx, gy = lax.axis_index("gx"), lax.axis_index("gy")
    nx_devices, ny_devices = counts

    def present(sx, sy):
        conditions = []
        if sx:
            conditions.append(gx > 0 if sx < 0 else gx < nx_devices - 1)
        if sy:
            conditions.append(gy > 0 if sy < 0 else gy < ny_devices - 1)
        return functools.reduce(jnp.logical_and, conditions)

    barrier = pltpu.get_barrier_semaphore()
    neighbours = 0
    for sx, sy in DIRECTIONS:
        there = present(sx, sy)
        neighbours = neighbours + there.astype(jnp.int32)

        @pl.when(there)
        def _():
            pl.semaphore_signal(
                barrier, inc=1, device_id=(parts_at, gx + sx, gy + sy), device_id_type=MESH
            )

    loads = [
        pltpu.make_async_copy(source, target, in_sem.at[n])
        for n, (source, target) in enumerate(
            (
                (cond_hbm, cond_in),
                (mass_hbm, mass_in),
                (res_hbm, res_in),
                (point_hbm, point_ref),
                (gen_hbm, gen_ref),
                (zoff_hbm, zoff_ref),
            )
        )
    ]
    for load in loads:
        load.start()
    for load in loads:
        load.wait()

    lane = lax.broadcasted_iota(jnp.int32, (8, LANES), 1)
    half = LANES // 2
    to_halves = jnp.where(lane < half, 2 * lane, 2 * lane - (LANES - 1))
    step = lane & 15
    to_strip = step + jnp.where(
        step < 4, half - 4, jnp.where(step < 8, LANES - 8, jnp.where(step < 12, -8, half - 12))
    )
    packs = [None] * 3
    for field in range(FIELDS):
        for pz in (0, 1):
            for px in (0, 1):
                t = 4 * field + 2 * pz + px
                for zc in (0, 1):
                    plane = 2 * zc + pz
                    if field < 3:
                        piece = cond_in[field, plane, pl.ds(px, 4, stride=2), :]
                    else:
                        source = mass_in if field == 3 else res_in
                        piece = source[plane, pl.ds(px, 4, stride=2), :]
                    own[t, pl.ds(zc, 4, stride=2), :] = piece
                halves = lanes_of(own[t], to_halves)
                own[t] = halves
                packed = lanes_of(halves, to_strip)
                word, group = divmod(t, 8)
                if packs[word] is None:
                    packs[word] = packed
                else:
                    packs[word] = jnp.where((lane >> 4) == group, packed, packs[word])
    for word in range(3):
        strip[word] = packs[word]

    pl.semaphore_wait(barrier, neighbours)

    def copy_to(n):
        sx, sy = DIRECTIONS[n]
        if sy == 0:
            source, target = own, side.at[0 if sx == 1 else 1]
        else:
            source, target = strip, strips.at[n]
        return pltpu.make_async_remote_copy(
            src_ref=source,
            dst_ref=target,
            send_sem=send_sem.at[n],
            recv_sem=recv_sem.at[n],
            device_id=(parts_at, gx + sx, gy + sy),
            device_id_type=MESH,
        )

    for n, (sx, sy) in enumerate(DIRECTIONS):
        @pl.when(present(sx, sy))
        def _():
            copy_to(n).start()

    own_copy = pltpu.make_async_copy(own, own_hbm, out_sem.at[0])
    own_copy.start()
    roots = field_roots(point_ref, gen_ref, zoff_ref, *place_of(counts, widths))
    for n, cls in enumerate(CLASSES):
        roots_out[n] = roots[cls]
    roots_copy = pltpu.make_async_copy(roots_out, roots_hbm, out_sem.at[1])
    roots_copy.start()

    for n, (sx, sy) in enumerate(DIRECTIONS):
        @pl.when(present(-sx, -sy))
        def _():
            copy_to(n).wait_recv()

        @pl.when(present(sx, sy))
        def _():
            copy_to(n).wait_send()
    own_copy.wait()
    roots_copy.wait()


def assemble(own, side, strips, wide):
    lane = lax.broadcasted_iota(jnp.int32, (8, LANES), 1)
    half = LANES // 2
    step = lane & 15
    merged = []
    for from_x in (-1, 0, 1):
        from_low = strips.at[DIRECTIONS.index((-from_x, 1))]
        from_high = strips.at[DIRECTIONS.index((-from_x, -1))]
        merged.append([jnp.where(step < 8, from_low[w], from_high[w]) for w in range(3)])
    for t in range(4 * FIELDS):
        word, group = divmod(t, 8)
        for block in range(3):
            tile = (side.at[0], own, side.at[1])[block][t]
            strip_tile = merged[block][word]
            for py in (0, 1):
                index = 16 * group + 4 * py + jnp.where(lane < half + 8, lane - half + 8, lane - (LANES - 4))
                index = jnp.where((lane >= half) & ((lane < half + 4) | (lane >= LANES - 4)), index, 0)
                edge = lanes_of(strip_tile, index)
                middle = pltpu.roll(tile, half, 1) if py else tile
                wide[2 * t + py, pl.ds(8 * block, 8), :] = jnp.where(lane < half, middle, edge)


def setup(
    counts, widths, own_hbm, side_hbm, strips_hbm, roots_hbm, stencil_hbm, solution_hbm,
    own, side, strips, roots_ref, wide, rows_out, stencil_out, solution_out, in_sem, sem,
):
    loads = [
        pltpu.make_async_copy(source, target, in_sem.at[n])
        for n, (source, target) in enumerate(
            ((own_hbm, own), (side_hbm, side), (strips_hbm, strips), (roots_hbm, roots_ref))
        )
    ]
    for load in loads:
        load.start()
    for load in loads:
        load.wait()
    assemble(own, side, strips, wide)

    def base(field, cls):
        return wide[8 * field + 4 * cls[0] + 2 * cls[1] + cls[2]]

    half = LANES // 2
    roots = {cls: roots_ref[n] for n, cls in enumerate(CLASSES)}
    cond, mass, residual = coefficients(base, roots, *place_of(counts, widths))
    stencil, rhs = galerkin(cond, mass, residual)
    for (dz, dx, dy), value in stencil.items():
        rows_out[9 * (dz + 1) + 3 * (dx + 1) + (dy + 1)] = value[8:16]
    for zc in (0, 1):
        for d in range(27):
            stencil_out[d, zc] = rows_out[d, pl.ds(zc, 4, stride=2), :][:, :half]
    stencil_copy = pltpu.make_async_copy(stencil_out, stencil_hbm, sem.at[0])
    stencil_copy.start()
    rows_out[27] = sweep_all(stencil, rhs)[8:16]
    for zc in (0, 1):
        solution_out[zc] = rows_out[27, pl.ds(zc, 4, stride=2), :][:, :half]
    solution_copy = pltpu.make_async_copy(solution_out, solution_hbm, sem.at[1])
    solution_copy.start()
    stencil_copy.wait()
    solution_copy.wait()


def solution(mesh):
    counts = (mesh.shape["gx"], mesh.shape["gy"])

    def on_device(base_cond, base_mass, fine_residual, point_index, gen_vector, z_offset):
        planes, width_x, width_y = base_mass.shape
        assert (planes, width_x, width_y) == (4, 8, LANES)
        tiles = 4 * FIELDS
        widths = (width_x, width_y)
        row_shape = (tiles, 8, LANES)
        moved = (row_shape, (2,) + row_shape, (8, 3, 8, LANES), (8, ROWS, LANES))
        whole = pl.BlockSpec(memory_space=pltpu.HBM)
        between = pl.pallas_call(
            functools.partial(exchange, counts, widths),
            out_shape=tuple(jax.ShapeDtypeStruct(shape, jnp.float32) for shape in moved),
            in_specs=[whole] * 6,
            out_specs=[whole] * 4,
            scratch_shapes=[
                pltpu.VMEM((3, planes, width_x, width_y), jnp.float32),
                pltpu.VMEM((planes, width_x, width_y), jnp.float32),
                pltpu.VMEM((planes, width_x, width_y), jnp.float32),
                pltpu.SMEM((1, 1), jnp.int32),
                pltpu.SMEM((MODES,), jnp.int32),
                pltpu.SMEM((1, 1), jnp.int32),
                pltpu.VMEM(row_shape, jnp.float32),
                pltpu.VMEM((3, 8, LANES), jnp.float32),
                pltpu.VMEM((8, ROWS, LANES), jnp.float32),
                pltpu.SemaphoreType.DMA((6,)),
                pltpu.SemaphoreType.DMA((8,)),
                pltpu.SemaphoreType.DMA((8,)),
                pltpu.SemaphoreType.DMA((2,)),
            ],
            compiler_params=pltpu.CompilerParams(
                collective_id=0, has_side_effects=True, vmem_limit_bytes=VMEM_GRANT
            ),
            name="exchange",
        )(
            base_cond, base_mass, fine_residual,
            point_index.reshape(1, 1), gen_vector, z_offset.reshape(1, 1),
        )
        out_planes, out_x, out_y = planes // 2, width_x // 2, width_y // 2
        stencil_shape, solution_shape = (27, out_planes, out_x, out_y), (out_planes, out_x, out_y)
        return pl.pallas_call(
            functools.partial(setup, counts, widths),
            out_shape=(
                jax.ShapeDtypeStruct(stencil_shape, jnp.float32),
                jax.ShapeDtypeStruct(solution_shape, jnp.float32),
            ),
            in_specs=[whole] * 4,
            out_specs=[whole] * 2,
            scratch_shapes=[pltpu.VMEM(shape, jnp.float32) for shape in moved]
            + [
                pltpu.VMEM((2 * tiles, ROWS, LANES), jnp.float32),
                pltpu.VMEM((28, 8, LANES), jnp.float32),
                pltpu.VMEM(stencil_shape, jnp.float32),
                pltpu.VMEM(solution_shape, jnp.float32),
                pltpu.SemaphoreType.DMA((4,)),
                pltpu.SemaphoreType.DMA((2,)),
            ],
            compiler_params=pltpu.CompilerParams(vmem_limit_bytes=VMEM_GRANT),
            name="setup",
        )(*between)

    return jax.shard_map(
        on_device,
        mesh=mesh,
        in_specs=(
            P(None, None, "gx", "gy"),
            P(None, "gx", "gy"),
            P("parts", "gx", "gy"),
            P("parts"),
            P(),
            P(),
        ),
        out_specs=(P(None, "parts", "gx", "gy"), P("parts", "gx", "gy")),
        check_vma=False,
    )
```

```python
import functools
import itertools
import math

import jax
import jax.numpy as jnp
from jax import lax
from jax.experimental import pallas as pl
from jax.experimental.pallas import tpu as pltpu
from jax.sharding import PartitionSpec as P

MESH = pl.DeviceIdType.MESH
NZG = 512
QMCN = 1048576
SWEEPS = 4
OMEGA = 0.6
MODES = 32
HALO = 4
CLASSES = list(itertools.product((0, 1), repeat=3))
FIELDS = 5
AXIS_FIELD = (2, 0, 1)
DIRECTIONS = [(sx, sy) for sx in (-1, 0, 1) for sy in (-1, 0, 1) if (sx, sy) != (0, 0)]
ROWS = 24
LANES = 128
VMEM_GRANT = 60 * 1024 * 1024


def cos_turns(turns):
    rest = 0.25 - jnp.abs(turns - jnp.round(turns))
    angle = rest * (2.0 * math.pi)
    square = angle * angle
    series = 1.0 / 6227020800.0
    for term in (-1.0 / 39916800.0, 1.0 / 362880.0, -1.0 / 5040.0, 1.0 / 120.0, -1.0 / 6.0, 1.0):
        series = series * square + term
    return series * angle


def shift(value, axis, step):
    if axis == 2:
        return pltpu.roll(value, (-step) % LANES, 1)
    return pltpu.roll(value, (-step * (1, 2)[axis]) % ROWS, 0)


def lanes_of(value, index):
    return jnp.take_along_axis(value, index, axis=1, mode="promise_in_bounds")


def flip(cls, axis):
    return tuple(1 - p if a == axis else p for a, p in enumerate(cls))


def field_roots(point_ref, gen_ref, zoff_ref, x_first, y_first, nx_total, ny_total):
    point = point_ref[0, 0]
    lane = lax.broadcasted_iota(jnp.int32, (1, 2 * MODES), 1)
    mode = jnp.where(lane < MODES, lane, lane - MODES)
    shifts = jnp.zeros((1, 2 * MODES), jnp.int32)
    for k in range(MODES):
        shifts = jnp.where(mode == k, (point * gen_ref[k]) & (QMCN - 1), shifts)
    modef = mode.astype(jnp.float32)
    amplitude = (shifts.astype(jnp.float32) / QMCN - 0.5) * (1.2 / (1.0 + 0.5 * modef))
    freq_z = modef - 5.0 * jnp.floor((modef + 0.5) * 0.2)
    freq_x = (1 + (mode & 3)).astype(jnp.float32)
    phase = modef * (0.7 / (2.0 * math.pi)) - jnp.where(lane < MODES, 0.0, 0.25)
    row = lax.broadcasted_iota(jnp.int32, (ROWS, 1), 0)
    z_row = (zoff_ref[0, 0] + 2 * (row & 1)).astype(jnp.float32) + 0.5
    x_row = (x_first + 2 * ((row >> 1) - HALO)).astype(jnp.float32) + 0.5
    left = []
    for pz, px in itertools.product((0, 1), repeat=2):
        turns = (z_row + pz) * (freq_z / (2.0 * NZG)) + (x_row + px) * (freq_x / (2.0 * nx_total))
        left.append(amplitude * cos_turns(turns + phase))
    left = jnp.concatenate(left, axis=0)
    mode_row = lax.broadcasted_iota(jnp.int32, (2 * MODES, 1), 0)
    freq_y = (1 + ((mode_row >> 2) & 3)).astype(jnp.float32)
    quarter = jnp.where(mode_row < MODES, 0.0, 0.25)
    place = lax.broadcasted_iota(jnp.int32, (1, LANES), 1)
    coarse = jnp.where(place < LANES // 2 + HALO, place, place - LANES)
    right = []
    for py in (0, 1):
        y_place = (y_first + 2 * coarse + py).astype(jnp.float32) + 0.5
        right.append(cos_turns(freq_y * (y_place / (2.0 * ny_total)) + quarter))
    right = jnp.concatenate(right, axis=1)
    logs = jnp.dot(left, right, precision=lax.Precision.HIGHEST, preferred_element_type=jnp.float32)
    roots = jnp.exp(0.5 * logs)
    out = {}
    for n, (pz, px) in enumerate(itertools.product((0, 1), repeat=2)):
        for py in (0, 1):
            out[pz, px, py] = roots[n * ROWS:(n + 1) * ROWS, py * LANES:(py + 1) * LANES]
    return out


def coefficients(base, roots, x_first, y_first, nx_total, ny_total):
    row = lax.broadcasted_iota(jnp.int32, (ROWS, LANES), 0)
    place = lax.broadcasted_iota(jnp.int32, (ROWS, LANES), 1)
    x_even = x_first + 2 * ((row >> 1) - HALO)
    half = LANES // 2
    y_even = y_first + 2 * jnp.where(place < half + HALO, place, place - LANES)
    inside = (x_even >= 0) & (x_even < nx_total) & (y_even >= 0) & (y_even < ny_total)
    inside = inside & ((place < half + HALO) | (place >= LANES - HALO))
    closed = (
        inside & ((row & 1) == 0),
        inside & (x_even + 2 < nx_total),
        inside & (y_even + 2 < ny_total),
    )
    cond, mass, residual = {}, {}, {}
    for cls in CLASSES:
        for axis in range(3):
            other = roots[flip(cls, axis)]
            if cls[axis]:
                other = shift(other, axis, 1)
            value = base(AXIS_FIELD[axis], cls) * roots[cls] * other
            cond[axis, cls] = jnp.where(closed[axis] if cls[axis] else inside, value, 0.0)
        mass[cls] = jnp.where(inside, base(3, cls) * (roots[cls] * roots[cls]), 1.0)
        residual[cls] = jnp.where(inside, base(4, cls), 0.0)
    return cond, mass, residual


def galerkin(cond, mass, residual):
    low = {}
    for cls in CLASSES:
        for axis in range(3):
            own = cond[axis, flip(cls, axis)]
            low[axis, cls] = own if cls[axis] else shift(own, axis, -1)

    weight = {((0, 0, 0), (0, 0, 0)): None}
    for cls in sorted(CLASSES, key=sum)[1:]:
        odd = [a for a in range(3) if cls[a]]
        total = mass[cls]
        for a in odd:
            total = total + (low[a, cls] + cond[a, cls])
        recip = 1.0 / total
        for corner in itertools.product(*[(0, 1) if p else (0,) for p in cls]):
            summed = None
            for a in odd:
                face = cond[a, cls] if corner[a] else low[a, cls]
                part = weight[flip(cls, a), tuple(0 if b == a else s for b, s in enumerate(corner))]
                if part is None:
                    term = face
                else:
                    term = face * (shift(part, a, 1) if corner[a] else part)
                summed = term if summed is None else summed + term
            weight[cls, corner] = recip * summed

    def wanted(offset):
        return offset >= (0, 0, 0)

    parts = {}

    def add(corner, offset, value):
        slot = parts.setdefault(offset, {})
        slot[corner] = slot[corner] + value if corner in slot else value

    for cls in sorted(CLASSES, key=sum)[:-1]:
        even = [a for a in range(3) if not cls[a]]
        pairs = None
        for a in even:
            pair = low[a, cls] + cond[a, cls]
            pairs = pair if pairs is None else pairs + pair
        if sum(cls) == 0:
            pairs = pairs + mass[cls]
        corners = list(itertools.product(*[(0, 1) if p else (0,) for p in cls]))
        applied = {}
        for corner in corners:
            own = weight[cls, corner]
            centre = pairs if own is None else pairs * own
            for a in even:
                up = flip(cls, a)
                high = tuple(1 if b == a else s for b, s in enumerate(corner))
                to_low = cond[a, up] * weight[up, corner]
                to_high = cond[a, up] * weight[up, high]
                centre = centre - shift(to_high, a, -1) - cond[a, cls] * weight[up, corner]
                below = tuple(-1 if b == a else s for b, s in enumerate(corner))
                applied[below] = -shift(to_low, a, -1)
                applied[high] = -(cond[a, cls] * weight[up, high])
            applied[corner] = centre
        for corner in corners:
            own = weight[cls, corner]
            for target, value in applied.items():
                offset = tuple(t - s for t, s in zip(target, corner))
                if wanted(offset):
                    add(corner, offset, value if own is None else own * value)

    def collect(slot):
        for axis in range(3):
            merged = {}
            for corner, value in slot.items():
                if corner[axis] == 0:
                    merged[corner] = merged[corner] + value if corner in merged else value
            for corner, value in slot.items():
                if corner[axis] == 1:
                    key = tuple(0 if b == axis else s for b, s in enumerate(corner))
                    moved = shift(value, axis, -1)
                    merged[key] = merged[key] + moved if key in merged else moved
            slot = merged
        return slot[0, 0, 0]

    stencil = {offset: collect(slot) for offset, slot in parts.items()}
    for offset in list(stencil):
        if offset != (0, 0, 0):
            value = stencil[offset]
            for axis, step in enumerate(offset):
                if step:
                    value = shift(value, axis, -step)
            stencil[tuple(-o for o in offset)] = value

    slot = {(0, 0, 0): residual[0, 0, 0]}
    for (cls, corner), own in weight.items():
        if own is not None:
            term = own * residual[cls]
            slot[corner] = slot[corner] + term if corner in slot else term
    return stencil, collect(slot)


def sweep_all(stencil, rhs):
    row = lax.broadcasted_iota(jnp.int32, (ROWS, LANES), 0)
    place = lax.broadcasted_iota(jnp.int32, (ROWS, LANES), 1)
    reach = HALO - 1
    valid = (row >= 2) & (row < ROWS - 2)
    valid = valid & ((place < LANES // 2 + reach) | (place >= LANES - reach))
    scale = jnp.where(valid, OMEGA / jnp.where(valid, stencil[0, 0, 0], 1.0), 0.0)
    values = rhs * scale
    for _ in range(SWEEPS - 1):
        rest = rhs
        for dz in (-1, 0, 1):
            in_z = shift(values, 0, dz) if dz else values
            for dx in (-1, 0, 1):
                in_x = shift(in_z, 1, dx) if dx else in_z
                for dy in (-1, 0, 1):
                    in_y = shift(in_x, 2, dy) if dy else in_x
                    rest = rest - stencil[dz, dx, dy] * in_y
        values = values + rest * scale
    return values


def place_of(counts, widths):
    gx, gy = lax.axis_index("gx"), lax.axis_index("gy")
    (nx_devices, ny_devices), (width_x, width_y) = counts, widths
    return gx * width_x, gy * width_y, nx_devices * width_x, ny_devices * width_y


def tiles_of(planes_of, staging):
    for field in range(FIELDS):
        for pz, px in itertools.product((0, 1), repeat=2):
            t = 4 * field + 2 * pz + px
            for zc in (0, 1):
                piece = planes_of(field, 2 * zc + pz, pl.ds(px, 4, stride=2))
                staging[t, pl.ds(zc, 4, stride=2), :] = piece


def own_planes(cond, mass, residual):
    def planes_of(field, plane, rows):
        if field < 3:
            return cond[field, plane, rows, :]
        return (mass if field == 3 else residual)[plane, rows, :]

    return planes_of


def exchange(
    counts, widths, cond_hbm, mass_hbm, res_hbm, point_hbm, gen_hbm, zoff_hbm,
    side, lows, highs, roots_hbm,
    cond_in, mass_in, res_in, point_ref, gen_ref, zoff_ref, own, low, high, roots_out,
    in_sem, send_sem, recv_sem, out_sem,
):
    parts_at = lax.axis_index("parts")
    gx, gy = lax.axis_index("gx"), lax.axis_index("gy")
    nx_devices, ny_devices = counts

    def present(sx, sy):
        conditions = []
        if sx:
            conditions.append(gx > 0 if sx < 0 else gx < nx_devices - 1)
        if sy:
            conditions.append(gy > 0 if sy < 0 else gy < ny_devices - 1)
        return functools.reduce(jnp.logical_and, conditions)

    barrier = pltpu.get_barrier_semaphore()
    neighbours = 0
    for sx, sy in DIRECTIONS:
        there = present(sx, sy)
        neighbours = neighbours + there.astype(jnp.int32)

        @pl.when(there)
        def _():
            pl.semaphore_signal(
                barrier, inc=1, device_id=(parts_at, gx + sx, gy + sy), device_id_type=MESH
            )

    loads = [
        pltpu.make_async_copy(source, target, in_sem.at[n])
        for n, (source, target) in enumerate(
            (
                (cond_hbm, cond_in),
                (mass_hbm, mass_in),
                (res_hbm, res_in),
                (point_hbm, point_ref),
                (gen_hbm, gen_ref),
                (zoff_hbm, zoff_ref),
            )
        )
    ]
    for load in loads:
        load.start()

    messages = []
    for sx in (1, -1):
        block = side.at[0 if sx == 1 else 1]
        messages += [
            ((sx, 0), cond_hbm.at[pl.ds(0, 2)], block.at[pl.ds(0, 2)]),
            ((sx, 0), cond_hbm.at[2, pl.ds(0, 3)], block.at[2, pl.ds(0, 3)]),
            ((sx, 0), mass_hbm, block.at[3]),
            ((sx, 0), res_hbm, block.at[4]),
        ]
    raw = len(messages)
    for sx in (1, -1, 0):
        messages += [((sx, 1), low, lows.at[1 - sx]), ((sx, -1), high, highs.at[1 - sx])]

    def message(n):
        (sx, sy), source, target = messages[n]
        return pltpu.make_async_remote_copy(
            src_ref=source,
            dst_ref=target,
            send_sem=send_sem.at[n],
            recv_sem=recv_sem.at[n],
            device_id=(parts_at, gx + sx, gy + sy),
            device_id_type=MESH,
        )

    def send(first, last):
        for direction in dict.fromkeys(m[0] for m in messages[first:last]):
            @pl.when(present(*direction))
            def _():
                for n in range(first, last):
                    if messages[n][0] == direction:
                        message(n).start()

    pl.semaphore_wait(barrier, neighbours)
    send(0, raw)

    for load in loads:
        load.wait()
    lane = lax.broadcasted_iota(jnp.int32, (8, LANES), 1)
    tiles_of(own_planes(cond_in, mass_in, res_in), own)
    from_last = LANES - 8 + (lane & 7)
    group = (lane * 171) >> 10
    from_first = lane - 6 * group
    packed_low, packed_high = [None, None], None
    for t in range(4 * FIELDS):
        tile = own[t]
        word, place = divmod(t, LANES // 8)
        last, first = lanes_of(tile, from_last), lanes_of(tile, from_first)
        packed_low[word] = last if place == 0 else jnp.where((lane >> 3) == place, last, packed_low[word])
        packed_high = first if t == 0 else jnp.where(group == t, first, packed_high)
    low[0], low[1] = packed_low
    high[...] = packed_high
    send(raw, len(messages))

    roots = field_roots(point_ref, gen_ref, zoff_ref, *place_of(counts, widths))
    for n, cls in enumerate(CLASSES):
        roots_out[n] = roots[cls]
    roots_copy = pltpu.make_async_copy(roots_out, roots_hbm, out_sem.at[0])
    roots_copy.start()

    for direction in dict.fromkeys(m[0] for m in messages):
        mine = [n for n in range(len(messages)) if messages[n][0] == direction]

        @pl.when(present(-direction[0], -direction[1]))
        def _():
            for n in mine:
                message(n).wait_recv()

        @pl.when(present(*direction))
        def _():
            for n in mine:
                message(n).wait_send()

    roots_copy.wait()


def assemble(tiles, lows, highs, wide):
    lane = lax.broadcasted_iota(jnp.int32, (8, LANES), 1)
    half = LANES // 2
    upper = lane >= LANES - HALO
    for t in range(4 * FIELDS):
        word, place = divmod(t, LANES // 8)
        for block in range(3):
            tile = tiles[block, t]
            for py in (0, 1):
                middle = lanes_of(tile, jnp.where(lane < half, 2 * lane + py, 0))
                low_index = jnp.where(upper, 8 * place + py + 2 * (lane - (LANES - HALO)), 0)
                high_index = jnp.where(
                    (lane >= half) & (lane < half + 3), 6 * t + py + 2 * (lane - half), 0
                )
                edge = jnp.where(
                    upper, lanes_of(lows[block, word], low_index), lanes_of(highs[block], high_index)
                )
                wide[2 * t + py, pl.ds(8 * block, 8), :] = jnp.where(lane < half, middle, edge)


def setup(
    counts, widths, cond_hbm, mass_hbm, res_hbm, side_hbm, lows_hbm, highs_hbm, roots_hbm,
    stencil_hbm, solution_hbm,
    cond_in, mass_in, res_in, side, lows, highs, roots_ref,
    tiles, wide, rows_out, stencil_out, solution_out, in_sem, sem,
):
    loads = [
        pltpu.make_async_copy(source, target, in_sem.at[n])
        for n, (source, target) in enumerate(
            (
                (cond_hbm, cond_in),
                (mass_hbm, mass_in),
                (res_hbm, res_in),
                (side_hbm, side),
                (lows_hbm, lows),
                (highs_hbm, highs),
                (roots_hbm, roots_ref),
            )
        )
    ]
    for load in loads:
        load.start()
    for load in loads:
        load.wait()
    tiles_of(lambda field, plane, rows: side[0, field, plane, rows, :], tiles.at[0])
    tiles_of(own_planes(cond_in, mass_in, res_in), tiles.at[1])
    tiles_of(lambda field, plane, rows: side[1, field, plane, rows, :], tiles.at[2])
    assemble(tiles, lows, highs, wide)

    def base(field, cls):
        return wide[8 * field + 4 * cls[0] + 2 * cls[1] + cls[2]]

    half = LANES // 2
    roots = {cls: roots_ref[n] for n, cls in enumerate(CLASSES)}
    cond, mass, residual = coefficients(base, roots, *place_of(counts, widths))
    stencil, rhs = galerkin(cond, mass, residual)
    for (dz, dx, dy), value in stencil.items():
        rows_out[9 * (dz + 1) + 3 * (dx + 1) + (dy + 1)] = value[8:16]
    for zc in (0, 1):
        for d in range(27):
            stencil_out[d, zc] = rows_out[d, pl.ds(zc, 4, stride=2), :][:, :half]
    stencil_copy = pltpu.make_async_copy(stencil_out, stencil_hbm, sem.at[0])
    stencil_copy.start()
    rows_out[27] = sweep_all(stencil, rhs)[8:16]
    for zc in (0, 1):
        solution_out[zc] = rows_out[27, pl.ds(zc, 4, stride=2), :][:, :half]
    solution_copy = pltpu.make_async_copy(solution_out, solution_hbm, sem.at[1])
    solution_copy.start()
    stencil_copy.wait()
    solution_copy.wait()


def solution(mesh):
    counts = (mesh.shape["gx"], mesh.shape["gy"])

    def on_device(base_cond, base_mass, fine_residual, point_index, gen_vector, z_offset):
        planes, width_x, width_y = base_mass.shape
        assert (planes, width_x, width_y) == (4, 8, LANES)
        tiles = 4 * FIELDS
        widths = (width_x, width_y)
        row_shape = (tiles, 8, LANES)
        inputs = [pltpu.VMEM(v.shape, jnp.float32) for v in (base_cond, base_mass, fine_residual)]
        moved = (
            (2, FIELDS, planes, width_x, width_y),
            (3, 2, 8, LANES),
            (3, 8, LANES),
            (8, ROWS, LANES),
        )
        whole = pl.BlockSpec(memory_space=pltpu.HBM)
        between = pl.pallas_call(
            functools.partial(exchange, counts, widths),
            out_shape=tuple(jax.ShapeDtypeStruct(shape, jnp.float32) for shape in moved),
            in_specs=[whole] * 6,
            out_specs=[whole] * 4,
            scratch_shapes=inputs
            + [
                pltpu.SMEM((1, 1), jnp.int32),
                pltpu.SMEM((MODES,), jnp.int32),
                pltpu.SMEM((1, 1), jnp.int32),
                pltpu.VMEM(row_shape, jnp.float32),
                pltpu.VMEM((2, 8, LANES), jnp.float32),
                pltpu.VMEM((8, LANES), jnp.float32),
                pltpu.VMEM((8, ROWS, LANES), jnp.float32),
                pltpu.SemaphoreType.DMA((6,)),
                pltpu.SemaphoreType.DMA((14,)),
                pltpu.SemaphoreType.DMA((14,)),
                pltpu.SemaphoreType.DMA((1,)),
            ],
            compiler_params=pltpu.CompilerParams(
                collective_id=0, has_side_effects=True, vmem_limit_bytes=VMEM_GRANT
            ),
            name="exchange",
        )(
            base_cond, base_mass, fine_residual,
            point_index.reshape(1, 1), gen_vector, z_offset.reshape(1, 1),
        )
        out_planes, out_x, out_y = planes // 2, width_x // 2, width_y // 2
        stencil_shape, solution_shape = (27, out_planes, out_x, out_y), (out_planes, out_x, out_y)
        return pl.pallas_call(
            functools.partial(setup, counts, widths),
            out_shape=(
                jax.ShapeDtypeStruct(stencil_shape, jnp.float32),
                jax.ShapeDtypeStruct(solution_shape, jnp.float32),
            ),
            in_specs=[whole] * 7,
            out_specs=[whole] * 2,
            scratch_shapes=inputs
            + [pltpu.VMEM(shape, jnp.float32) for shape in moved]
            + [
                pltpu.VMEM((3,) + row_shape, jnp.float32),
                pltpu.VMEM((2 * tiles, ROWS, LANES), jnp.float32),
                pltpu.VMEM((28, 8, LANES), jnp.float32),
                pltpu.VMEM(stencil_shape, jnp.float32),
                pltpu.VMEM(solution_shape, jnp.float32),
                pltpu.SemaphoreType.DMA((7,)),
                pltpu.SemaphoreType.DMA((2,)),
            ],
            compiler_params=pltpu.CompilerParams(vmem_limit_bytes=VMEM_GRANT),
            name="setup",
        )(base_cond, base_mass, fine_residual, *between)

    return jax.shard_map(
        on_device,
        mesh=mesh,
        in_specs=(
            P(None, None, "gx", "gy"),
            P(None, "gx", "gy"),
            P("parts", "gx", "gy"),
            P("parts"),
            P(),
            P(),
        ),
        out_specs=(P(None, "parts", "gx", "gy"), P("parts", "gx", "gy")),
        check_vma=False,
    )
```

```python
import functools
import itertools
import math

import jax
import jax.numpy as jnp
from jax import lax
from jax.experimental import pallas as pl
from jax.experimental.pallas import tpu as pltpu
from jax.sharding import PartitionSpec as P

MESH = pl.DeviceIdType.MESH
NZG = 512
QMCN = 1048576
SWEEPS = 4
OMEGA = 0.6
MODES = 32
HALO = 4
CLASSES = list(itertools.product((0, 1), repeat=3))
FIELDS = 5
AXIS_FIELD = (2, 0, 1)
DIRECTIONS = [(sx, sy) for sx in (-1, 0, 1) for sy in (-1, 0, 1) if (sx, sy) != (0, 0)]
ROWS = 24
LANES = 128
VMEM_GRANT = 60 * 1024 * 1024


def cos_turns(turns):
    rest = 0.25 - jnp.abs(turns - jnp.round(turns))
    angle = rest * (2.0 * math.pi)
    square = angle * angle
    series = 1.0 / 6227020800.0
    for term in (-1.0 / 39916800.0, 1.0 / 362880.0, -1.0 / 5040.0, 1.0 / 120.0, -1.0 / 6.0, 1.0):
        series = series * square + term
    return series * angle


def shift(value, axis, step):
    if axis == 2:
        return pltpu.roll(value, (-step) % LANES, 1)
    return pltpu.roll(value, (-step * (1, 2)[axis]) % ROWS, 0)


def lanes_of(value, index):
    return jnp.take_along_axis(value, index, axis=1, mode="promise_in_bounds")


def flip(cls, axis):
    return tuple(1 - p if a == axis else p for a, p in enumerate(cls))


def split_lanes(tile, index):
    return lanes_of(tile, index)


def halves_of(value):
    high = value.astype(jnp.bfloat16)
    return high, (value - high.astype(jnp.float32)).astype(jnp.bfloat16)


def field_roots(scalars, x_first, y_first, nx_total, ny_total):
    half = MODES // 2
    point_ref, gen_ref, zoff_ref = scalars
    point = point_ref[0, 0]
    lane = lax.broadcasted_iota(jnp.int32, (1, 2 * MODES), 1)
    mode = (lane & (half - 1)) + jnp.where(lane < MODES, 0, half)
    shifts = jnp.zeros((1, 2 * MODES), jnp.int32)
    for k in range(MODES):
        shifts = jnp.where(mode == k, (point * gen_ref[k]) & (QMCN - 1), shifts)
    modef = mode.astype(jnp.float32)
    amplitude = (shifts.astype(jnp.float32) / QMCN - 0.5) * (1.2 / (1.0 + 0.5 * modef))
    freq_z = modef - 5.0 * jnp.floor((modef + 0.5) * 0.2)
    freq_x = (1 + (mode & 3)).astype(jnp.float32)
    phase = modef * (0.7 / (2.0 * math.pi)) - jnp.where((lane & half) == 0, 0.0, 0.25)
    row = lax.broadcasted_iota(jnp.int32, (ROWS, 1), 0)
    z_row = (zoff_ref[0, 0] + 2 * (row & 1)).astype(jnp.float32) + 0.5
    x_row = (x_first + 2 * ((row >> 1) - HALO)).astype(jnp.float32) + 0.5
    left = []
    for pz, px in itertools.product((0, 1), repeat=2):
        turns = (z_row + pz) * (freq_z / (2.0 * NZG)) + (x_row + px) * (freq_x / (2.0 * nx_total))
        left.append(amplitude * cos_turns(turns + phase))
    left = jnp.concatenate(left, axis=0)
    left = left[:, :MODES] + left[:, MODES:]
    mode_row = lax.broadcasted_iota(jnp.int32, (MODES, 1), 0)
    freq_y = (1 + ((mode_row >> 2) & 3)).astype(jnp.float32)
    quarter = jnp.where(mode_row < half, 0.0, 0.25)
    place = lax.broadcasted_iota(jnp.int32, (1, LANES), 1)
    coarse = jnp.where(place < LANES // 2 + HALO, place, place - LANES)
    right = []
    for py in (0, 1):
        y_place = (y_first + 2 * coarse + py).astype(jnp.float32) + 0.5
        right.append(cos_turns(freq_y * (y_place / (2.0 * ny_total)) + quarter))
    right = jnp.concatenate(right, axis=1)
    left_high, left_low = halves_of(left)
    right_high, right_low = halves_of(right)
    logs = jnp.dot(
        jnp.concatenate([left_high, left_high, left_low], axis=1),
        jnp.concatenate([right_high, right_low, right_high], axis=0),
        preferred_element_type=jnp.float32,
    )
    roots = jnp.exp(0.5 * logs)
    out = {}
    for n, (pz, px) in enumerate(itertools.product((0, 1), repeat=2)):
        for py in (0, 1):
            out[pz, px, py] = roots[n * ROWS:(n + 1) * ROWS, py * LANES:(py + 1) * LANES]
    return out


def coefficients(base, roots, x_first, y_first, nx_total, ny_total):
    row = lax.broadcasted_iota(jnp.int32, (ROWS, LANES), 0)
    place = lax.broadcasted_iota(jnp.int32, (ROWS, LANES), 1)
    x_even = x_first + 2 * ((row >> 1) - HALO)
    half = LANES // 2
    y_even = y_first + 2 * jnp.where(place < half + HALO, place, place - LANES)
    inside = (x_even >= 0) & (x_even < nx_total) & (y_even >= 0) & (y_even < ny_total)
    inside = inside & ((place < half + HALO) | (place >= LANES - HALO))
    closed = (
        inside & ((row & 1) == 0),
        inside & (x_even + 2 < nx_total),
        inside & (y_even + 2 < ny_total),
    )
    cond, mass, residual = {}, {}, {}
    for cls in CLASSES:
        for axis in range(3):
            other = roots[flip(cls, axis)]
            if cls[axis]:
                other = shift(other, axis, 1)
            value = base(AXIS_FIELD[axis], cls) * roots[cls] * other
            cond[axis, cls] = jnp.where(closed[axis] if cls[axis] else inside, value, 0.0)
        mass[cls] = jnp.where(inside, base(3, cls) * (roots[cls] * roots[cls]), 1.0)
        residual[cls] = jnp.where(inside, base(4, cls), 0.0)
    return cond, mass, residual


def galerkin(cond, mass, residual):
    low = {}
    for cls in CLASSES:
        for axis in range(3):
            own = cond[axis, flip(cls, axis)]
            low[axis, cls] = own if cls[axis] else shift(own, axis, -1)

    weight = {((0, 0, 0), (0, 0, 0)): None}
    for cls in sorted(CLASSES, key=sum)[1:]:
        odd = [a for a in range(3) if cls[a]]
        total = mass[cls]
        for a in odd:
            total = total + (low[a, cls] + cond[a, cls])
        recip = 1.0 / total
        for corner in itertools.product(*[(0, 1) if p else (0,) for p in cls]):
            summed = None
            for a in odd:
                face = cond[a, cls] if corner[a] else low[a, cls]
                part = weight[flip(cls, a), tuple(0 if b == a else s for b, s in enumerate(corner))]
                if part is None:
                    term = face
                else:
                    term = face * (shift(part, a, 1) if corner[a] else part)
                summed = term if summed is None else summed + term
            weight[cls, corner] = recip * summed

    def wanted(offset):
        return offset >= (0, 0, 0)

    parts = {}

    def add(corner, offset, value):
        slot = parts.setdefault(offset, {})
        slot[corner] = slot[corner] + value if corner in slot else value

    for cls in sorted(CLASSES, key=sum)[:-1]:
        even = [a for a in range(3) if not cls[a]]
        pairs = None
        for a in even:
            pair = low[a, cls] + cond[a, cls]
            pairs = pair if pairs is None else pairs + pair
        if sum(cls) == 0:
            pairs = pairs + mass[cls]
        corners = list(itertools.product(*[(0, 1) if p else (0,) for p in cls]))
        applied = {}
        for corner in corners:
            own = weight[cls, corner]
            centre = pairs if own is None else pairs * own
            for a in even:
                up = flip(cls, a)
                high = tuple(1 if b == a else s for b, s in enumerate(corner))
                to_low = cond[a, up] * weight[up, corner]
                to_high = cond[a, up] * weight[up, high]
                centre = centre - shift(to_high, a, -1) - cond[a, cls] * weight[up, corner]
                below = tuple(-1 if b == a else s for b, s in enumerate(corner))
                applied[below] = -shift(to_low, a, -1)
                applied[high] = -(cond[a, cls] * weight[up, high])
            applied[corner] = centre
        for corner in corners:
            own = weight[cls, corner]
            for target, value in applied.items():
                offset = tuple(t - s for t, s in zip(target, corner))
                if wanted(offset):
                    add(corner, offset, value if own is None else own * value)

    def collect(slot):
        for axis in range(3):
            merged = {}
            for corner, value in slot.items():
                if corner[axis] == 0:
                    merged[corner] = merged[corner] + value if corner in merged else value
            for corner, value in slot.items():
                if corner[axis] == 1:
                    key = tuple(0 if b == axis else s for b, s in enumerate(corner))
                    moved = shift(value, axis, -1)
                    merged[key] = merged[key] + moved if key in merged else moved
            slot = merged
        return slot[0, 0, 0]

    stencil = {offset: collect(slot) for offset, slot in parts.items()}
    for offset in list(stencil):
        if offset != (0, 0, 0):
            value = stencil[offset]
            for axis, step in enumerate(offset):
                if step:
                    value = shift(value, axis, -step)
            stencil[tuple(-o for o in offset)] = value

    slot = {(0, 0, 0): residual[0, 0, 0]}
    for (cls, corner), own in weight.items():
        if own is not None:
            term = own * residual[cls]
            slot[corner] = slot[corner] + term if corner in slot else term
    return stencil, collect(slot)


def sweep_all(stencil, rhs):
    row = lax.broadcasted_iota(jnp.int32, (ROWS, LANES), 0)
    place = lax.broadcasted_iota(jnp.int32, (ROWS, LANES), 1)
    reach = HALO - 1
    valid = (row >= 2) & (row < ROWS - 2)
    valid = valid & ((place < LANES // 2 + reach) | (place >= LANES - reach))
    scale = jnp.where(valid, OMEGA / jnp.where(valid, stencil[0, 0, 0], 1.0), 0.0)
    values = rhs * scale
    for _ in range(SWEEPS - 1):
        rest = rhs
        for dz in (-1, 0, 1):
            in_z = shift(values, 0, dz) if dz else values
            for dx in (-1, 0, 1):
                in_x = shift(in_z, 1, dx) if dx else in_z
                for dy in (-1, 0, 1):
                    in_y = shift(in_x, 2, dy) if dy else in_x
                    rest = rest - stencil[dz, dx, dy] * in_y
        values = values + rest * scale
    return values


def place_of(counts, widths):
    gx, gy = lax.axis_index("gx"), lax.axis_index("gy")
    (nx_devices, ny_devices), (width_x, width_y) = counts, widths
    return gx * width_x, gy * width_y, nx_devices * width_x, ny_devices * width_y


def exchange(
    counts, widths, cond_hbm, mass_hbm, res_hbm, point_hbm, gen_hbm, zoff_hbm,
    own_hbm, side, strips, roots_hbm,
    cond_in, mass_in, res_in, point_ref, gen_ref, zoff_ref, own, low, high, roots_out,
    in_sem, send_sem, recv_sem, out_sem,
):
    parts_at = lax.axis_index("parts")
    gx, gy = lax.axis_index("gx"), lax.axis_index("gy")
    nx_devices, ny_devices = counts

    def present(sx, sy):
        conditions = []
        if sx:
            conditions.append(gx > 0 if sx < 0 else gx < nx_devices - 1)
        if sy:
            conditions.append(gy > 0 if sy < 0 else gy < ny_devices - 1)
        return functools.reduce(jnp.logical_and, conditions)

    barrier = pltpu.get_barrier_semaphore()
    neighbours = 0
    for sx, sy in DIRECTIONS:
        there = present(sx, sy)
        neighbours = neighbours + there.astype(jnp.int32)

        @pl.when(there)
        def _():
            pl.semaphore_signal(
                barrier, inc=1, device_id=(parts_at, gx + sx, gy + sy), device_id_type=MESH
            )

    loads = [
        pltpu.make_async_copy(source, target, in_sem.at[n])
        for n, (source, target) in enumerate(
            (
                (cond_hbm, cond_in),
                (mass_hbm, mass_in),
                (res_hbm, res_in),
                (point_hbm, point_ref),
                (gen_hbm, gen_ref),
                (zoff_hbm, zoff_ref),
            )
        )
    ]
    for load in loads:
        load.start()
    for load in loads:
        load.wait()

    lane = lax.broadcasted_iota(jnp.int32, (8, LANES), 1)
    half = LANES // 2
    to_halves = jnp.where(lane < half, 2 * lane, 2 * lane - (LANES - 1))
    step = lane & 7
    to_low = step + jnp.where(step < 4, half - 4, LANES - 8)
    to_high = step + jnp.where(step < 4, 0, half - 4)
    packs = [None] * 4
    for field in range(FIELDS):
        for pz in (0, 1):
            for px in (0, 1):
                t = 4 * field + 2 * pz + px
                for zc in (0, 1):
                    plane = 2 * zc + pz
                    if field < 3:
                        piece = cond_in[field, plane, pl.ds(px, 4, stride=2), :]
                    else:
                        source = mass_in if field == 3 else res_in
                        piece = source[plane, pl.ds(px, 4, stride=2), :]
                    own[t, pl.ds(zc, 4, stride=2), :] = piece
                halves = lanes_of(own[t], to_halves)
                own[t] = halves
                word, place = divmod(t, 16)
                for slot, packed in (
                    (word, lanes_of(halves, to_low)),
                    (2 + word, lanes_of(halves, to_high)),
                ):
                    if place:
                        packed = jnp.where((lane >> 3) == place, packed, packs[slot])
                    packs[slot] = packed
    for word in (0, 1):
        low[word], high[word] = packs[word], packs[2 + word]

    pl.semaphore_wait(barrier, neighbours)

    def copy_to(n):
        sx, sy = DIRECTIONS[n]
        if sy == 0:
            source, target = own, side.at[0 if sx == 1 else 1]
        else:
            source, target = low if sy == 1 else high, strips.at[n]
        return pltpu.make_async_remote_copy(
            src_ref=source,
            dst_ref=target,
            send_sem=send_sem.at[n],
            recv_sem=recv_sem.at[n],
            device_id=(parts_at, gx + sx, gy + sy),
            device_id_type=MESH,
        )

    for n, (sx, sy) in enumerate(DIRECTIONS):
        @pl.when(present(sx, sy))
        def _():
            copy_to(n).start()

    own_copy = pltpu.make_async_copy(own, own_hbm, out_sem.at[0])
    own_copy.start()
    roots = field_roots((point_ref, gen_ref, zoff_ref), *place_of(counts, widths))
    for n, cls in enumerate(CLASSES):
        roots_out[n] = roots[cls]
    roots_copy = pltpu.make_async_copy(roots_out, roots_hbm, out_sem.at[1])
    roots_copy.start()

    for n, (sx, sy) in enumerate(DIRECTIONS):
        @pl.when(present(-sx, -sy))
        def _():
            copy_to(n).wait_recv()

        @pl.when(present(sx, sy))
        def _():
            copy_to(n).wait_send()
    own_copy.wait()
    roots_copy.wait()


def assemble(own, side, strips, wide):
    lane = lax.broadcasted_iota(jnp.int32, (8, LANES), 1)
    half = LANES // 2
    even = (lane & 8) == 0
    merged = []
    for from_x in (-1, 0, 1):
        from_low = strips.at[DIRECTIONS.index((-from_x, 1))]
        from_high = strips.at[DIRECTIONS.index((-from_x, -1))]
        words = []
        for word in (0, 1):
            low, high = from_low[word], from_high[word]
            words.append(
                (
                    jnp.where(even, low, pltpu.roll(high, 8, 1)),
                    jnp.where(even, pltpu.roll(low, LANES - 8, 1), high),
                )
            )
        merged.append(words)
    for t in range(4 * FIELDS):
        word, place = divmod(t, 16)
        group, odd = divmod(place, 2)
        for block in range(3):
            tile = (side.at[0], own, side.at[1])[block][t]
            strip_tile = merged[block][word][odd]
            for py in (0, 1):
                index = 16 * group + 4 * py + jnp.where(lane < half + 8, lane - half + 8, lane - (LANES - 4))
                index = jnp.where((lane >= half) & ((lane < half + 4) | (lane >= LANES - 4)), index, 0)
                edge = lanes_of(strip_tile, index)
                middle = pltpu.roll(tile, half, 1) if py else tile
                wide[2 * t + py, pl.ds(8 * block, 8), :] = jnp.where(lane < half, middle, edge)


def setup(
    counts, widths, own_hbm, side_hbm, strips_hbm, roots_hbm, stencil_hbm, solution_hbm,
    own, side, strips, roots_ref, wide, rows_out, stencil_out, solution_out, in_sem, sem,
):
    loads = [
        pltpu.make_async_copy(source, target, in_sem.at[n])
        for n, (source, target) in enumerate(
            ((own_hbm, own), (side_hbm, side), (strips_hbm, strips), (roots_hbm, roots_ref))
        )
    ]
    for load in loads:
        load.start()
    for load in loads:
        load.wait()
    assemble(own, side, strips, wide)

    def base(field, cls):
        return wide[8 * field + 4 * cls[0] + 2 * cls[1] + cls[2]]

    half = LANES // 2
    roots = {cls: roots_ref[n] for n, cls in enumerate(CLASSES)}
    cond, mass, residual = coefficients(base, roots, *place_of(counts, widths))
    stencil, rhs = galerkin(cond, mass, residual)
    for (dz, dx, dy), value in stencil.items():
        rows_out[9 * (dz + 1) + 3 * (dx + 1) + (dy + 1)] = value[8:16]
    for zc in (0, 1):
        for d in range(27):
            stencil_out[d, zc] = rows_out[d, pl.ds(zc, 4, stride=2), :][:, :half]
    stencil_copy = pltpu.make_async_copy(stencil_out, stencil_hbm, sem.at[0])
    stencil_copy.start()
    rows_out[27] = sweep_all(stencil, rhs)[8:16]
    for zc in (0, 1):
        solution_out[zc] = rows_out[27, pl.ds(zc, 4, stride=2), :][:, :half]
    solution_copy = pltpu.make_async_copy(solution_out, solution_hbm, sem.at[1])
    solution_copy.start()
    stencil_copy.wait()
    solution_copy.wait()


def solution(mesh):
    counts = (mesh.shape["gx"], mesh.shape["gy"])

    def on_device(base_cond, base_mass, fine_residual, point_index, gen_vector, z_offset):
        planes, width_x, width_y = base_mass.shape
        assert (planes, width_x, width_y) == (4, 8, LANES)
        tiles = 4 * FIELDS
        widths = (width_x, width_y)
        row_shape = (tiles, 8, LANES)
        moved = (row_shape, (2,) + row_shape, (8, 2, 8, LANES), (8, ROWS, LANES))
        whole = pl.BlockSpec(memory_space=pltpu.HBM)
        between = pl.pallas_call(
            functools.partial(exchange, counts, widths),
            out_shape=tuple(jax.ShapeDtypeStruct(shape, jnp.float32) for shape in moved),
            in_specs=[whole] * 6,
            out_specs=[whole] * 4,
            scratch_shapes=[
                pltpu.VMEM((3, planes, width_x, width_y), jnp.float32),
                pltpu.VMEM((planes, width_x, width_y), jnp.float32),
                pltpu.VMEM((planes, width_x, width_y), jnp.float32),
                pltpu.SMEM((1, 1), jnp.int32),
                pltpu.SMEM((MODES,), jnp.int32),
                pltpu.SMEM((1, 1), jnp.int32),
                pltpu.VMEM(row_shape, jnp.float32),
                pltpu.VMEM((2, 8, LANES), jnp.float32),
                pltpu.VMEM((2, 8, LANES), jnp.float32),
                pltpu.VMEM((8, ROWS, LANES), jnp.float32),
                pltpu.SemaphoreType.DMA((6,)),
                pltpu.SemaphoreType.DMA((8,)),
                pltpu.SemaphoreType.DMA((8,)),
                pltpu.SemaphoreType.DMA((2,)),
            ],
            compiler_params=pltpu.CompilerParams(
                collective_id=0, has_side_effects=True, vmem_limit_bytes=VMEM_GRANT
            ),
            name="exchange",
        )(
            base_cond, base_mass, fine_residual,
            point_index.reshape(1, 1), gen_vector, z_offset.reshape(1, 1),
        )
        out_planes, out_x, out_y = planes // 2, width_x // 2, width_y // 2
        stencil_shape, solution_shape = (27, out_planes, out_x, out_y), (out_planes, out_x, out_y)
        return pl.pallas_call(
            functools.partial(setup, counts, widths),
            out_shape=(
                jax.ShapeDtypeStruct(stencil_shape, jnp.float32),
                jax.ShapeDtypeStruct(solution_shape, jnp.float32),
            ),
            in_specs=[whole] * 4,
            out_specs=[whole] * 2,
            scratch_shapes=[pltpu.VMEM(shape, jnp.float32) for shape in moved]
            + [
                pltpu.VMEM((2 * tiles, ROWS, LANES), jnp.float32),
                pltpu.VMEM((28, 8, LANES), jnp.float32),
                pltpu.VMEM(stencil_shape, jnp.float32),
                pltpu.VMEM(solution_shape, jnp.float32),
                pltpu.SemaphoreType.DMA((4,)),
                pltpu.SemaphoreType.DMA((2,)),
            ],
            compiler_params=pltpu.CompilerParams(vmem_limit_bytes=VMEM_GRANT),
            name="setup",
        )(*between)

    return jax.shard_map(
        on_device,
        mesh=mesh,
        in_specs=(
            P(None, None, "gx", "gy"),
            P(None, "gx", "gy"),
            P("parts", "gx", "gy"),
            P("parts"),
            P(),
            P(),
        ),
        out_specs=(P(None, "parts", "gx", "gy"), P("parts", "gx", "gy")),
        check_vma=False,
    )
```

```python
import functools
import itertools
import math

import jax
import jax.numpy as jnp
from jax import lax
from jax.experimental import pallas as pl
from jax.experimental.pallas import tpu as pltpu
from jax.sharding import PartitionSpec as P

MESH = pl.DeviceIdType.MESH
NZG = 512
QMCN = 1048576
SWEEPS = 4
OMEGA = 0.6
MODES = 32
HALO = 4
CLASSES = list(itertools.product((0, 1), repeat=3))
FIELDS = 5
AXIS_FIELD = (2, 0, 1)
DIRECTIONS = [(1, 0), (-1, 0), (0, 1), (0, -1), (1, 1), (1, -1), (-1, 1), (-1, -1)]
CORNERS = DIRECTIONS[4:]
STRIP = 60
ROWS = 24
LANES = 128
VMEM_GRANT = 60 * 1024 * 1024


def cos_turns(turns):
    rest = 0.25 - jnp.abs(turns - jnp.round(turns))
    angle = rest * (2.0 * math.pi)
    square = angle * angle
    series = 1.0 / 6227020800.0
    for term in (-1.0 / 39916800.0, 1.0 / 362880.0, -1.0 / 5040.0, 1.0 / 120.0, -1.0 / 6.0, 1.0):
        series = series * square + term
    return series * angle


def shift(value, axis, step):
    if axis == 2:
        return pltpu.roll(value, (-step) % LANES, 1)
    return pltpu.roll(value, (-step * (1, 2)[axis]) % ROWS, 0)


def lanes_of(value, index):
    return jnp.take_along_axis(value, index, axis=1, mode="promise_in_bounds")


def flip(cls, axis):
    return tuple(1 - p if a == axis else p for a, p in enumerate(cls))


def split_lanes(tile, index):
    return lanes_of(tile, index)


def halves_of(value):
    high = value.astype(jnp.bfloat16)
    return high, (value - high.astype(jnp.float32)).astype(jnp.bfloat16)


def field_roots(scalars, x_first, y_first, nx_total, ny_total):
    half = MODES // 2
    point_ref, gen_ref, zoff_ref = scalars
    point = point_ref[0, 0]
    lane = lax.broadcasted_iota(jnp.int32, (1, 2 * MODES), 1)
    mode = (lane & (half - 1)) + jnp.where(lane < MODES, 0, half)
    shifts = jnp.zeros((1, 2 * MODES), jnp.int32)
    for k in range(MODES):
        shifts = jnp.where(mode == k, (point * gen_ref[k]) & (QMCN - 1), shifts)
    modef = mode.astype(jnp.float32)
    amplitude = (shifts.astype(jnp.float32) / QMCN - 0.5) * (1.2 / (1.0 + 0.5 * modef))
    freq_z = modef - 5.0 * jnp.floor((modef + 0.5) * 0.2)
    freq_x = (1 + (mode & 3)).astype(jnp.float32)
    phase = modef * (0.7 / (2.0 * math.pi)) - jnp.where((lane & half) == 0, 0.0, 0.25)
    row = lax.broadcasted_iota(jnp.int32, (ROWS, 1), 0)
    z_row = (zoff_ref[0, 0] + 2 * (row & 1)).astype(jnp.float32) + 0.5
    x_row = (x_first + 2 * ((row >> 1) - HALO)).astype(jnp.float32) + 0.5
    left = []
    for pz, px in itertools.product((0, 1), repeat=2):
        turns = (z_row + pz) * (freq_z / (2.0 * NZG)) + (x_row + px) * (freq_x / (2.0 * nx_total))
        left.append(amplitude * cos_turns(turns + phase))
    left = jnp.concatenate(left, axis=0)
    left = left[:, :MODES] + left[:, MODES:]
    mode_row = lax.broadcasted_iota(jnp.int32, (MODES, 1), 0)
    freq_y = (1 + ((mode_row >> 2) & 3)).astype(jnp.float32)
    quarter = jnp.where(mode_row < half, 0.0, 0.25)
    place = lax.broadcasted_iota(jnp.int32, (1, LANES), 1)
    coarse = jnp.where(place < LANES // 2 + HALO, place, place - LANES)
    right = []
    for py in (0, 1):
        y_place = (y_first + 2 * coarse + py).astype(jnp.float32) + 0.5
        right.append(cos_turns(freq_y * (y_place / (2.0 * ny_total)) + quarter))
    right = jnp.concatenate(right, axis=1)
    left_high, left_low = halves_of(left)
    right_high, right_low = halves_of(right)
    logs = jnp.dot(
        jnp.concatenate([left_high, left_high, left_low], axis=1),
        jnp.concatenate([right_high, right_low, right_high], axis=0),
        preferred_element_type=jnp.float32,
    )
    roots = jnp.exp(0.5 * logs)
    out = {}
    for n, (pz, px) in enumerate(itertools.product((0, 1), repeat=2)):
        for py in (0, 1):
            out[pz, px, py] = roots[n * ROWS:(n + 1) * ROWS, py * LANES:(py + 1) * LANES]
    return out


def coefficients(base, roots, x_first, y_first, nx_total, ny_total):
    row = lax.broadcasted_iota(jnp.int32, (ROWS, LANES), 0)
    place = lax.broadcasted_iota(jnp.int32, (ROWS, LANES), 1)
    x_even = x_first + 2 * ((row >> 1) - HALO)
    half = LANES // 2
    y_even = y_first + 2 * jnp.where(place < half + HALO, place, place - LANES)
    inside = (x_even >= 0) & (x_even < nx_total) & (y_even >= 0) & (y_even < ny_total)
    inside = inside & ((place < half + HALO) | (place >= LANES - HALO))
    closed = (
        inside & ((row & 1) == 0),
        inside & (x_even + 2 < nx_total),
        inside & (y_even + 2 < ny_total),
    )
    cond, mass, residual = {}, {}, {}
    for cls in CLASSES:
        for axis in range(3):
            other = roots[flip(cls, axis)]
            if cls[axis]:
                other = shift(other, axis, 1)
            value = base(AXIS_FIELD[axis], cls) * roots[cls] * other
            cond[axis, cls] = jnp.where(closed[axis] if cls[axis] else inside, value, 0.0)
        mass[cls] = jnp.where(inside, base(3, cls) * (roots[cls] * roots[cls]), 1.0)
        residual[cls] = jnp.where(inside, base(4, cls), 0.0)
    return cond, mass, residual


def galerkin(cond, mass, residual):
    low = {}
    for cls in CLASSES:
        for axis in range(3):
            own = cond[axis, flip(cls, axis)]
            low[axis, cls] = own if cls[axis] else shift(own, axis, -1)

    weight = {((0, 0, 0), (0, 0, 0)): None}
    for cls in sorted(CLASSES, key=sum)[1:]:
        odd = [a for a in range(3) if cls[a]]
        total = mass[cls]
        for a in odd:
            total = total + (low[a, cls] + cond[a, cls])
        recip = 1.0 / total
        for corner in itertools.product(*[(0, 1) if p else (0,) for p in cls]):
            summed = None
            for a in odd:
                face = cond[a, cls] if corner[a] else low[a, cls]
                part = weight[flip(cls, a), tuple(0 if b == a else s for b, s in enumerate(corner))]
                if part is None:
                    term = face
                else:
                    term = face * (shift(part, a, 1) if corner[a] else part)
                summed = term if summed is None else summed + term
            weight[cls, corner] = recip * summed

    def wanted(offset):
        return offset >= (0, 0, 0)

    parts = {}

    def add(corner, offset, value):
        slot = parts.setdefault(offset, {})
        slot[corner] = slot[corner] + value if corner in slot else value

    for cls in sorted(CLASSES, key=sum)[:-1]:
        even = [a for a in range(3) if not cls[a]]
        pairs = None
        for a in even:
            pair = low[a, cls] + cond[a, cls]
            pairs = pair if pairs is None else pairs + pair
        if sum(cls) == 0:
            pairs = pairs + mass[cls]
        corners = list(itertools.product(*[(0, 1) if p else (0,) for p in cls]))
        applied = {}
        for corner in corners:
            own = weight[cls, corner]
            centre = pairs if own is None else pairs * own
            for a in even:
                up = flip(cls, a)
                high = tuple(1 if b == a else s for b, s in enumerate(corner))
                to_low = cond[a, up] * weight[up, corner]
                to_high = cond[a, up] * weight[up, high]
                centre = centre - shift(to_high, a, -1) - cond[a, cls] * weight[up, corner]
                below = tuple(-1 if b == a else s for b, s in enumerate(corner))
                applied[below] = -shift(to_low, a, -1)
                applied[high] = -(cond[a, cls] * weight[up, high])
            applied[corner] = centre
        for corner in corners:
            own = weight[cls, corner]
            for target, value in applied.items():
                offset = tuple(t - s for t, s in zip(target, corner))
                if wanted(offset):
                    add(corner, offset, value if own is None else own * value)

    def collect(slot):
        for axis in range(3):
            merged = {}
            for corner, value in slot.items():
                if corner[axis] == 0:
                    merged[corner] = merged[corner] + value if corner in merged else value
            for corner, value in slot.items():
                if corner[axis] == 1:
                    key = tuple(0 if b == axis else s for b, s in enumerate(corner))
                    moved = shift(value, axis, -1)
                    merged[key] = merged[key] + moved if key in merged else moved
            slot = merged
        return slot[0, 0, 0]

    stencil = {offset: collect(slot) for offset, slot in parts.items()}
    for offset in list(stencil):
        if offset != (0, 0, 0):
            value = stencil[offset]
            for axis, step in enumerate(offset):
                if step:
                    value = shift(value, axis, -step)
            stencil[tuple(-o for o in offset)] = value

    slot = {(0, 0, 0): residual[0, 0, 0]}
    for (cls, corner), own in weight.items():
        if own is not None:
            term = own * residual[cls]
            slot[corner] = slot[corner] + term if corner in slot else term
    return stencil, collect(slot)


def sweep_all(stencil, rhs):
    row = lax.broadcasted_iota(jnp.int32, (ROWS, LANES), 0)
    place = lax.broadcasted_iota(jnp.int32, (ROWS, LANES), 1)
    reach = HALO - 1
    valid = (row >= 2) & (row < ROWS - 2)
    valid = valid & ((place < LANES // 2 + reach) | (place >= LANES - reach))
    scale = jnp.where(valid, OMEGA / jnp.where(valid, stencil[0, 0, 0], 1.0), 0.0)
    values = rhs * scale
    for _ in range(SWEEPS - 1):
        rest = rhs
        for dz in (-1, 0, 1):
            in_z = shift(values, 0, dz) if dz else values
            for dx in (-1, 0, 1):
                in_x = shift(in_z, 1, dx) if dx else in_z
                for dy in (-1, 0, 1):
                    in_y = shift(in_x, 2, dy) if dy else in_x
                    rest = rest - stencil[dz, dx, dy] * in_y
        values = values + rest * scale
    return values


def place_of(counts, widths):
    gx, gy = lax.axis_index("gx"), lax.axis_index("gy")
    (nx_devices, ny_devices), (width_x, width_y) = counts, widths
    return gx * width_x, gy * width_y, nx_devices * width_x, ny_devices * width_y


def exchange(
    counts, widths, cond_hbm, mass_hbm, res_hbm, point_hbm, gen_hbm, zoff_hbm,
    wide_hbm, side, strips, roots_hbm,
    cond_in, mass_in, res_in, point_ref, gen_ref, zoff_ref, own, strip, beside, wide, roots_out,
    in_sem, send_sem, recv_sem, out_sem,
):
    parts_at = lax.axis_index("parts")
    gx, gy = lax.axis_index("gx"), lax.axis_index("gy")
    nx_devices, ny_devices = counts

    def present(sx, sy):
        conditions = []
        if sx:
            conditions.append(gx > 0 if sx < 0 else gx < nx_devices - 1)
        if sy:
            conditions.append(gy > 0 if sy < 0 else gy < ny_devices - 1)
        return functools.reduce(jnp.logical_and, conditions)

    barrier = pltpu.get_barrier_semaphore()
    neighbours = 0
    for sx, sy in DIRECTIONS:
        there = present(sx, sy)
        neighbours = neighbours + there.astype(jnp.int32)

        @pl.when(there)
        def _():
            pl.semaphore_signal(
                barrier, inc=1, device_id=(parts_at, gx + sx, gy + sy), device_id_type=MESH
            )

    loads = [
        pltpu.make_async_copy(source, target, in_sem.at[n])
        for n, (source, target) in enumerate(
            (
                (cond_hbm, cond_in),
                (mass_hbm, mass_in),
                (res_hbm, res_in),
                (point_hbm, point_ref),
                (gen_hbm, gen_ref),
                (zoff_hbm, zoff_ref),
            )
        )
    ]
    for load in loads:
        load.start()
    for load in loads:
        load.wait()

    lane = lax.broadcasted_iota(jnp.int32, (8, LANES), 1)
    half = LANES // 2
    to_halves = jnp.where(lane < half, 2 * lane, 2 * lane - (LANES - 1))
    first, last = lane & 7, (lane - STRIP) & 7
    to_strip = jnp.where(
        lane < STRIP,
        first + jnp.where(first < 4, 0, half - 4),
        last + jnp.where(last < 4, half - 4, LANES - 8),
    )
    slot = jnp.where(lane < STRIP, lane >> 3, (lane - STRIP) >> 3)
    packs = [None] * 3
    for field in range(FIELDS):
        for pz in (0, 1):
            for px in (0, 1):
                t = 4 * field + 2 * pz + px
                for zc in (0, 1):
                    plane = 2 * zc + pz
                    if field < 3:
                        piece = cond_in[field, plane, pl.ds(px, 4, stride=2), :]
                    else:
                        source = mass_in if field == 3 else res_in
                        piece = source[plane, pl.ds(px, 4, stride=2), :]
                    own[t, pl.ds(zc, 4, stride=2), :] = piece
                halves = lanes_of(own[t], to_halves)
                own[t] = halves
                word, place = divmod(t, 7)
                packed = lanes_of(halves, to_strip)
                packs[word] = jnp.where(slot == place, packed, packs[word]) if place else packed
    for word in range(3):
        strip[word] = packs[word]

    pl.semaphore_wait(barrier, neighbours)

    def copy_to(n):
        sx, sy = DIRECTIONS[n]
        if sy == 0:
            source, target = own, side.at[0 if sx == 1 else 1]
        else:
            source = strip
            target = strips.at[n - 4] if sx else beside.at[0 if sy == 1 else 1]
        return pltpu.make_async_remote_copy(
            src_ref=source,
            dst_ref=target,
            send_sem=send_sem.at[n],
            recv_sem=recv_sem.at[n],
            device_id=(parts_at, gx + sx, gy + sy),
            device_id_type=MESH,
        )

    for n, (sx, sy) in enumerate(DIRECTIONS):
        @pl.when(present(sx, sy))
        def _():
            copy_to(n).start()

    roots = field_roots((point_ref, gen_ref, zoff_ref), *place_of(counts, widths))
    for n, cls in enumerate(CLASSES):
        roots_out[n] = roots[cls]
    roots_copy = pltpu.make_async_copy(roots_out, roots_hbm, out_sem.at[1])
    roots_copy.start()

    def finish(directions):
        for direction in directions:
            n = DIRECTIONS.index(direction)

            @pl.when(present(-direction[0], -direction[1]))
            def _():
                copy_to(n).wait_recv()

            @pl.when(present(*direction))
            def _():
                copy_to(n).wait_send()

    finish(DIRECTIONS[2:4])
    assemble(own, beside.at[0], beside.at[1], wide, 0)
    wide_copy = pltpu.make_async_copy(wide, wide_hbm, out_sem.at[0])
    wide_copy.start()
    finish(DIRECTIONS[:2] + CORNERS)
    roots_copy.wait()
    wide_copy.wait()


def assemble(tiles, from_low, from_high, wide, first_row):
    lane = lax.broadcasted_iota(jnp.int32, (8, LANES), 1)
    half = LANES // 2
    merged = [jnp.where(lane < STRIP, from_high[w], from_low[w]) for w in range(3)]
    for t in range(4 * FIELDS):
        tile = tiles[t]
        word, place = divmod(t, 7)
        for py in (0, 1):
            edge = pltpu.roll(merged[word], half - 8 * place - 4 * py, 1)
            middle = pltpu.roll(tile, half, 1) if py else tile
            wide[2 * t + py, pl.ds(first_row, 8), :] = jnp.where(lane < half, middle, edge)


def setup(
    counts, widths, wide_hbm, side_hbm, strips_hbm, roots_hbm, stencil_hbm, solution_hbm,
    side, strips, roots_ref, wide, rows_out, stencil_out, solution_out, in_sem, sem,
):
    loads = [
        pltpu.make_async_copy(source, target, in_sem.at[n])
        for n, (source, target) in enumerate(
            (
                (side_hbm, side),
                (strips_hbm, strips),
                (wide_hbm, wide.at[:, pl.ds(8, 8)]),
                (roots_hbm, roots_ref),
            )
        )
    ]
    for load in loads:
        load.start()
    for load in loads:
        load.wait()
    for block, sx in ((0, 1), (2, -1)):
        from_low, from_high = (strips.at[CORNERS.index((sx, sy))] for sy in (1, -1))
        assemble(side.at[block // 2], from_low, from_high, wide, 8 * block)

    def base(field, cls):
        return wide[8 * field + 4 * cls[0] + 2 * cls[1] + cls[2]]

    half = LANES // 2
    roots = {cls: roots_ref[n] for n, cls in enumerate(CLASSES)}
    cond, mass, residual = coefficients(base, roots, *place_of(counts, widths))
    stencil, rhs = galerkin(cond, mass, residual)
    for (dz, dx, dy), value in stencil.items():
        rows_out[9 * (dz + 1) + 3 * (dx + 1) + (dy + 1)] = value[8:16]
    for zc in (0, 1):
        for d in range(27):
            stencil_out[d, zc] = rows_out[d, pl.ds(zc, 4, stride=2), :][:, :half]
    stencil_copy = pltpu.make_async_copy(stencil_out, stencil_hbm, sem.at[0])
    stencil_copy.start()
    rows_out[27] = sweep_all(stencil, rhs)[8:16]
    for zc in (0, 1):
        solution_out[zc] = rows_out[27, pl.ds(zc, 4, stride=2), :][:, :half]
    solution_copy = pltpu.make_async_copy(solution_out, solution_hbm, sem.at[1])
    solution_copy.start()
    stencil_copy.wait()
    solution_copy.wait()


def solution(mesh):
    counts = (mesh.shape["gx"], mesh.shape["gy"])

    def on_device(base_cond, base_mass, fine_residual, point_index, gen_vector, z_offset):
        planes, width_x, width_y = base_mass.shape
        assert (planes, width_x, width_y) == (4, 8, LANES)
        tiles = 4 * FIELDS
        widths = (width_x, width_y)
        row_shape = (tiles, 8, LANES)
        own_wide = (2 * tiles, 8, LANES)
        moved = (own_wide, (2,) + row_shape, (4, 3, 8, LANES), (8, ROWS, LANES))
        whole = pl.BlockSpec(memory_space=pltpu.HBM)
        between = pl.pallas_call(
            functools.partial(exchange, counts, widths),
            out_shape=tuple(jax.ShapeDtypeStruct(shape, jnp.float32) for shape in moved),
            in_specs=[whole] * 6,
            out_specs=[whole] * 4,
            scratch_shapes=[
                pltpu.VMEM((3, planes, width_x, width_y), jnp.float32),
                pltpu.VMEM((planes, width_x, width_y), jnp.float32),
                pltpu.VMEM((planes, width_x, width_y), jnp.float32),
                pltpu.SMEM((1, 1), jnp.int32),
                pltpu.SMEM((MODES,), jnp.int32),
                pltpu.SMEM((1, 1), jnp.int32),
                pltpu.VMEM(row_shape, jnp.float32),
                pltpu.VMEM((3, 8, LANES), jnp.float32),
                pltpu.VMEM((2, 3, 8, LANES), jnp.float32),
                pltpu.VMEM(own_wide, jnp.float32),
                pltpu.VMEM((8, ROWS, LANES), jnp.float32),
                pltpu.SemaphoreType.DMA((6,)),
                pltpu.SemaphoreType.DMA((8,)),
                pltpu.SemaphoreType.DMA((8,)),
                pltpu.SemaphoreType.DMA((2,)),
            ],
            compiler_params=pltpu.CompilerParams(
                collective_id=0, has_side_effects=True, vmem_limit_bytes=VMEM_GRANT
            ),
            name="exchange",
        )(
            base_cond, base_mass, fine_residual,
            point_index.reshape(1, 1), gen_vector, z_offset.reshape(1, 1),
        )
        out_planes, out_x, out_y = planes // 2, width_x // 2, width_y // 2
        stencil_shape, solution_shape = (27, out_planes, out_x, out_y), (out_planes, out_x, out_y)
        return pl.pallas_call(
            functools.partial(setup, counts, widths),
            out_shape=(
                jax.ShapeDtypeStruct(stencil_shape, jnp.float32),
                jax.ShapeDtypeStruct(solution_shape, jnp.float32),
            ),
            in_specs=[whole] * 4,
            out_specs=[whole] * 2,
            scratch_shapes=[pltpu.VMEM(shape, jnp.float32) for shape in moved[1:]]
            + [
                pltpu.VMEM((2 * tiles, ROWS, LANES), jnp.float32),
                pltpu.VMEM((28, 8, LANES), jnp.float32),
                pltpu.VMEM(stencil_shape, jnp.float32),
                pltpu.VMEM(solution_shape, jnp.float32),
                pltpu.SemaphoreType.DMA((4,)),
                pltpu.SemaphoreType.DMA((2,)),
            ],
            compiler_params=pltpu.CompilerParams(vmem_limit_bytes=VMEM_GRANT),
            name="setup",
        )(*between)

    return jax.shard_map(
        on_device,
        mesh=mesh,
        in_specs=(
            P(None, None, "gx", "gy"),
            P(None, "gx", "gy"),
            P("parts", "gx", "gy"),
            P("parts"),
            P(),
            P(),
        ),
        out_specs=(P(None, "parts", "gx", "gy"), P("parts", "gx", "gy")),
        check_vma=False,
    )
```

```python
import functools
import itertools
import math

import jax
import jax.numpy as jnp
from jax import lax
from jax.experimental import pallas as pl
from jax.experimental.pallas import tpu as pltpu
from jax.sharding import PartitionSpec as P

MESH = pl.DeviceIdType.MESH
NZG = 512
QMCN = 1048576
SWEEPS = 4
OMEGA = 0.6
MODES = 32
HALO = 4
CLASSES = list(itertools.product((0, 1), repeat=3))
FIELDS = 5
AXIS_FIELD = (2, 0, 1)
CORNERS = [(1, 1), (1, -1), (-1, 1), (-1, -1)]
DIRECTIONS = CORNERS + [(0, 1), (0, -1), (1, 0), (-1, 0)]
STRIP = 60
ROWS = 24
LANES = 128
VMEM_GRANT = 60 * 1024 * 1024


def cos_turns(turns):
    rest = 0.25 - jnp.abs(turns - jnp.round(turns))
    angle = rest * (2.0 * math.pi)
    square = angle * angle
    series = 1.0 / 6227020800.0
    for term in (-1.0 / 39916800.0, 1.0 / 362880.0, -1.0 / 5040.0, 1.0 / 120.0, -1.0 / 6.0, 1.0):
        series = series * square + term
    return series * angle


def shift(value, axis, step):
    if axis == 2:
        return pltpu.roll(value, (-step) % LANES, 1)
    return pltpu.roll(value, (-step * (1, 2)[axis]) % ROWS, 0)


def lanes_of(value, index):
    return jnp.take_along_axis(value, index, axis=1, mode="promise_in_bounds")


def flip(cls, axis):
    return tuple(1 - p if a == axis else p for a, p in enumerate(cls))


def split_lanes(tile, index):
    return lanes_of(tile, index)


def halves_of(value):
    high = value.astype(jnp.bfloat16)
    return high, (value - high.astype(jnp.float32)).astype(jnp.bfloat16)


def field_roots(scalars, x_first, y_first, nx_total, ny_total):
    half = MODES // 2
    point_ref, gen_ref, zoff_ref = scalars
    point = point_ref[0, 0]
    lane = lax.broadcasted_iota(jnp.int32, (1, 2 * MODES), 1)
    mode = (lane & (half - 1)) + jnp.where(lane < MODES, 0, half)
    shifts = jnp.zeros((1, 2 * MODES), jnp.int32)
    for k in range(MODES):
        shifts = jnp.where(mode == k, (point * gen_ref[k]) & (QMCN - 1), shifts)
    modef = mode.astype(jnp.float32)
    amplitude = (shifts.astype(jnp.float32) / QMCN - 0.5) * (1.2 / (1.0 + 0.5 * modef))
    freq_z = modef - 5.0 * jnp.floor((modef + 0.5) * 0.2)
    freq_x = (1 + (mode & 3)).astype(jnp.float32)
    phase = modef * (0.7 / (2.0 * math.pi)) - jnp.where((lane & half) == 0, 0.0, 0.25)
    row = lax.broadcasted_iota(jnp.int32, (ROWS, 1), 0)
    z_row = (zoff_ref[0, 0] + 2 * (row & 1)).astype(jnp.float32) + 0.5
    x_row = (x_first + 2 * ((row >> 1) - HALO)).astype(jnp.float32) + 0.5
    left = []
    for pz, px in itertools.product((0, 1), repeat=2):
        turns = (z_row + pz) * (freq_z / (2.0 * NZG)) + (x_row + px) * (freq_x / (2.0 * nx_total))
        left.append(amplitude * cos_turns(turns + phase))
    left = jnp.concatenate(left, axis=0)
    left = left[:, :MODES] + left[:, MODES:]
    mode_row = lax.broadcasted_iota(jnp.int32, (MODES, 1), 0)
    freq_y = (1 + ((mode_row >> 2) & 3)).astype(jnp.float32)
    quarter = jnp.where(mode_row < half, 0.0, 0.25)
    place = lax.broadcasted_iota(jnp.int32, (1, LANES), 1)
    coarse = jnp.where(place < LANES // 2 + HALO, place, place - LANES)
    right = []
    for py in (0, 1):
        y_place = (y_first + 2 * coarse + py).astype(jnp.float32) + 0.5
        right.append(cos_turns(freq_y * (y_place / (2.0 * ny_total)) + quarter))
    right = jnp.concatenate(right, axis=1)
    left_high, left_low = halves_of(left)
    right_high, right_low = halves_of(right)
    logs = jnp.dot(
        jnp.concatenate([left_high, left_high, left_low], axis=1),
        jnp.concatenate([right_high, right_low, right_high], axis=0),
        preferred_element_type=jnp.float32,
    )
    roots = jnp.exp(0.5 * logs)
    out = {}
    for n, (pz, px) in enumerate(itertools.product((0, 1), repeat=2)):
        for py in (0, 1):
            out[pz, px, py] = roots[n * ROWS:(n + 1) * ROWS, py * LANES:(py + 1) * LANES]
    return out


def coefficients(base, roots, x_first, y_first, nx_total, ny_total):
    row = lax.broadcasted_iota(jnp.int32, (ROWS, LANES), 0)
    place = lax.broadcasted_iota(jnp.int32, (ROWS, LANES), 1)
    x_even = x_first + 2 * ((row >> 1) - HALO)
    half = LANES // 2
    y_even = y_first + 2 * jnp.where(place < half + HALO, place, place - LANES)
    inside = (x_even >= 0) & (x_even < nx_total) & (y_even >= 0) & (y_even < ny_total)
    inside = inside & ((place < half + HALO) | (place >= LANES - HALO))
    inside = inside & (row < ROWS - 2)
    closed = (
        inside & ((row & 1) == 0),
        inside & (x_even + 2 < nx_total),
        inside & (y_even + 2 < ny_total),
    )
    cond, mass, residual = {}, {}, {}
    for cls in CLASSES:
        for axis in range(3):
            other = roots[flip(cls, axis)]
            if cls[axis]:
                other = shift(other, axis, 1)
            value = base(AXIS_FIELD[axis], cls) * roots[cls] * other
            cond[axis, cls] = jnp.where(closed[axis] if cls[axis] else inside, value, 0.0)
        mass[cls] = jnp.where(inside, base(3, cls) * (roots[cls] * roots[cls]), 1.0)
        residual[cls] = jnp.where(inside, base(4, cls), 0.0)
    return cond, mass, residual


def galerkin(cond, mass, residual):
    low = {}
    for cls in CLASSES:
        for axis in range(3):
            own = cond[axis, flip(cls, axis)]
            low[axis, cls] = own if cls[axis] else shift(own, axis, -1)

    weight = {((0, 0, 0), (0, 0, 0)): None}
    for cls in sorted(CLASSES, key=sum)[1:]:
        odd = [a for a in range(3) if cls[a]]
        total = mass[cls]
        for a in odd:
            total = total + (low[a, cls] + cond[a, cls])
        recip = 1.0 / total
        for corner in itertools.product(*[(0, 1) if p else (0,) for p in cls]):
            summed = None
            for a in odd:
                face = cond[a, cls] if corner[a] else low[a, cls]
                part = weight[flip(cls, a), tuple(0 if b == a else s for b, s in enumerate(corner))]
                if part is None:
                    term = face
                else:
                    term = face * (shift(part, a, 1) if corner[a] else part)
                summed = term if summed is None else summed + term
            weight[cls, corner] = recip * summed

    def wanted(offset):
        return offset >= (0, 0, 0)

    parts = {}

    def add(corner, offset, value):
        slot = parts.setdefault(offset, {})
        slot[corner] = slot[corner] + value if corner in slot else value

    for cls in sorted(CLASSES, key=sum)[:-1]:
        even = [a for a in range(3) if not cls[a]]
        pairs = None
        for a in even:
            pair = low[a, cls] + cond[a, cls]
            pairs = pair if pairs is None else pairs + pair
        if sum(cls) == 0:
            pairs = pairs + mass[cls]
        corners = list(itertools.product(*[(0, 1) if p else (0,) for p in cls]))
        applied = {}
        for corner in corners:
            own = weight[cls, corner]
            centre = pairs if own is None else pairs * own
            for a in even:
                up = flip(cls, a)
                high = tuple(1 if b == a else s for b, s in enumerate(corner))
                to_low = cond[a, up] * weight[up, corner]
                to_high = cond[a, up] * weight[up, high]
                centre = centre - shift(to_high, a, -1) - cond[a, cls] * weight[up, corner]
                below = tuple(-1 if b == a else s for b, s in enumerate(corner))
                applied[below] = -shift(to_low, a, -1)
                applied[high] = -(cond[a, cls] * weight[up, high])
            applied[corner] = centre
        for corner in corners:
            own = weight[cls, corner]
            for target, value in applied.items():
                offset = tuple(t - s for t, s in zip(target, corner))
                if wanted(offset):
                    add(corner, offset, value if own is None else own * value)

    def collect(slot):
        for axis in range(3):
            merged = {}
            for corner, value in slot.items():
                if corner[axis] == 0:
                    merged[corner] = merged[corner] + value if corner in merged else value
            for corner, value in slot.items():
                if corner[axis] == 1:
                    key = tuple(0 if b == axis else s for b, s in enumerate(corner))
                    moved = shift(value, axis, -1)
                    merged[key] = merged[key] + moved if key in merged else moved
            slot = merged
        return slot[0, 0, 0]

    stencil = {offset: collect(slot) for offset, slot in parts.items()}
    for offset in list(stencil):
        if offset != (0, 0, 0):
            value = stencil[offset]
            for axis, step in enumerate(offset):
                if step:
                    value = shift(value, axis, -step)
            stencil[tuple(-o for o in offset)] = value

    slot = {(0, 0, 0): residual[0, 0, 0]}
    for (cls, corner), own in weight.items():
        if own is not None:
            term = own * residual[cls]
            slot[corner] = slot[corner] + term if corner in slot else term
    return stencil, collect(slot)


def sweep_all(stencil, rhs):
    row = lax.broadcasted_iota(jnp.int32, (ROWS, LANES), 0)
    place = lax.broadcasted_iota(jnp.int32, (ROWS, LANES), 1)
    reach = HALO - 1
    valid = (row >= 2) & (row < ROWS - 2)
    valid = valid & ((place < LANES // 2 + reach) | (place >= LANES - reach))
    scale = jnp.where(valid, OMEGA / jnp.where(valid, stencil[0, 0, 0], 1.0), 0.0)
    values = rhs * scale
    for _ in range(SWEEPS - 1):
        rest = rhs
        for dz in (-1, 0, 1):
            in_z = shift(values, 0, dz) if dz else values
            for dx in (-1, 0, 1):
                in_x = shift(in_z, 1, dx) if dx else in_z
                for dy in (-1, 0, 1):
                    in_y = shift(in_x, 2, dy) if dy else in_x
                    rest = rest - stencil[dz, dx, dy] * in_y
        values = values + rest * scale
    return values


def place_of(counts, widths):
    gx, gy = lax.axis_index("gx"), lax.axis_index("gy")
    (nx_devices, ny_devices), (width_x, width_y) = counts, widths
    return gx * width_x, gy * width_y, nx_devices * width_x, ny_devices * width_y


def exchange(
    counts, widths, cond_hbm, mass_hbm, res_hbm, point_hbm, gen_hbm, zoff_hbm,
    wide_hbm, side, strips, roots_hbm,
    cond_in, mass_in, res_in, point_ref, gen_ref, zoff_ref, own, strip, beside, wide, roots_out,
    in_sem, send_sem, recv_sem, out_sem,
):
    parts_at = lax.axis_index("parts")
    gx, gy = lax.axis_index("gx"), lax.axis_index("gy")
    nx_devices, ny_devices = counts

    def present(sx, sy):
        conditions = []
        if sx:
            conditions.append(gx > 0 if sx < 0 else gx < nx_devices - 1)
        if sy:
            conditions.append(gy > 0 if sy < 0 else gy < ny_devices - 1)
        return functools.reduce(jnp.logical_and, conditions)

    barrier = pltpu.get_barrier_semaphore()
    neighbours = 0
    for sx, sy in DIRECTIONS:
        there = present(sx, sy)
        neighbours = neighbours + there.astype(jnp.int32)

        @pl.when(there)
        def _():
            pl.semaphore_signal(
                barrier, inc=1, device_id=(parts_at, gx + sx, gy + sy), device_id_type=MESH
            )

    loads = [
        pltpu.make_async_copy(source, target, in_sem.at[n])
        for n, (source, target) in enumerate(
            (
                (cond_hbm, cond_in),
                (mass_hbm, mass_in),
                (res_hbm, res_in),
                (point_hbm, point_ref),
                (gen_hbm, gen_ref),
                (zoff_hbm, zoff_ref),
            )
        )
    ]
    for load in loads:
        load.start()
    for load in loads:
        load.wait()

    lane = lax.broadcasted_iota(jnp.int32, (8, LANES), 1)
    half = LANES // 2
    to_halves = jnp.where(lane < half, 2 * lane, 2 * lane - (LANES - 1))
    first, last = lane & 7, (lane - STRIP) & 7
    to_strip = jnp.where(
        lane < STRIP,
        first + jnp.where(first < 4, 0, half - 4),
        last + jnp.where(last < 4, half - 4, LANES - 8),
    )
    slot = jnp.where(lane < STRIP, lane >> 3, (lane - STRIP) >> 3)
    packs = [None] * 3
    for field in range(FIELDS):
        for pz in (0, 1):
            for px in (0, 1):
                t = 4 * field + 2 * pz + px
                for zc in (0, 1):
                    plane = 2 * zc + pz
                    if field < 3:
                        piece = cond_in[field, plane, pl.ds(px, 4, stride=2), :]
                    else:
                        source = mass_in if field == 3 else res_in
                        piece = source[plane, pl.ds(px, 4, stride=2), :]
                    own[t, pl.ds(zc, 4, stride=2), :] = piece
                halves = lanes_of(own[t], to_halves)
                own[t] = halves
                word, place = divmod(t, 7)
                packed = lanes_of(halves, to_strip)
                packs[word] = jnp.where(slot == place, packed, packs[word]) if place else packed
    for word in range(3):
        strip[word] = packs[word]

    pl.semaphore_wait(barrier, neighbours)

    def copy_to(n):
        sx, sy = DIRECTIONS[n]
        if sy == 0:
            source, target = own, side.at[0 if sx == 1 else 1]
            if sx == -1:
                source, target = source.at[:, pl.ds(0, 6)], target.at[:, pl.ds(0, 6)]
        else:
            source = strip
            target = strips.at[n] if sx else beside.at[0 if sy == 1 else 1]
        return pltpu.make_async_remote_copy(
            src_ref=source,
            dst_ref=target,
            send_sem=send_sem.at[n],
            recv_sem=recv_sem.at[n],
            device_id=(parts_at, gx + sx, gy + sy),
            device_id_type=MESH,
        )

    for n, (sx, sy) in enumerate(DIRECTIONS):
        @pl.when(present(sx, sy))
        def _():
            copy_to(n).start()

    roots = field_roots((point_ref, gen_ref, zoff_ref), *place_of(counts, widths))
    for n, cls in enumerate(CLASSES):
        roots_out[n] = roots[cls]
    roots_copy = pltpu.make_async_copy(roots_out, roots_hbm, out_sem.at[1])
    roots_copy.start()

    def finish(directions):
        for direction in directions:
            n = DIRECTIONS.index(direction)

            @pl.when(present(-direction[0], -direction[1]))
            def _():
                copy_to(n).wait_recv()

            @pl.when(present(*direction))
            def _():
                copy_to(n).wait_send()

    finish(DIRECTIONS[4:6])
    assemble(own, beside.at[0], beside.at[1], wide, 0)
    wide_copy = pltpu.make_async_copy(wide, wide_hbm, out_sem.at[0])
    wide_copy.start()
    finish(CORNERS + DIRECTIONS[6:])
    roots_copy.wait()
    wide_copy.wait()


def assemble(tiles, from_low, from_high, wide, first_row):
    lane = lax.broadcasted_iota(jnp.int32, (8, LANES), 1)
    half = LANES // 2
    merged = [jnp.where(lane < STRIP, from_high[w], from_low[w]) for w in range(3)]
    for t in range(4 * FIELDS):
        tile = tiles[t]
        word, place = divmod(t, 7)
        for py in (0, 1):
            edge = pltpu.roll(merged[word], half - 8 * place - 4 * py, 1)
            middle = pltpu.roll(tile, half, 1) if py else tile
            wide[2 * t + py, pl.ds(first_row, 8), :] = jnp.where(lane < half, middle, edge)


def setup(
    counts, widths, wide_hbm, side_hbm, strips_hbm, roots_hbm, stencil_hbm, solution_hbm,
    side, strips, roots_ref, wide, rows_out, stencil_out, solution_out, in_sem, sem,
):
    loads = [
        pltpu.make_async_copy(source, target, in_sem.at[n])
        for n, (source, target) in enumerate(
            (
                (side_hbm, side),
                (strips_hbm, strips),
                (wide_hbm, wide.at[:, pl.ds(8, 8)]),
                (roots_hbm, roots_ref),
            )
        )
    ]
    for load in loads:
        load.start()
    for load in loads:
        load.wait()
    for block, sx in ((0, 1), (2, -1)):
        from_low, from_high = (strips.at[CORNERS.index((sx, sy))] for sy in (1, -1))
        assemble(side.at[block // 2], from_low, from_high, wide, 8 * block)

    def base(field, cls):
        return wide[8 * field + 4 * cls[0] + 2 * cls[1] + cls[2]]

    half = LANES // 2
    roots = {cls: roots_ref[n] for n, cls in enumerate(CLASSES)}
    cond, mass, residual = coefficients(base, roots, *place_of(counts, widths))
    stencil, rhs = galerkin(cond, mass, residual)
    for (dz, dx, dy), value in stencil.items():
        rows_out[9 * (dz + 1) + 3 * (dx + 1) + (dy + 1)] = value[8:16]
    for zc in (0, 1):
        for d in range(27):
            stencil_out[d, zc] = rows_out[d, pl.ds(zc, 4, stride=2), :][:, :half]
    stencil_copy = pltpu.make_async_copy(stencil_out, stencil_hbm, sem.at[0])
    stencil_copy.start()
    rows_out[27] = sweep_all(stencil, rhs)[8:16]
    for zc in (0, 1):
        solution_out[zc] = rows_out[27, pl.ds(zc, 4, stride=2), :][:, :half]
    solution_copy = pltpu.make_async_copy(solution_out, solution_hbm, sem.at[1])
    solution_copy.start()
    stencil_copy.wait()
    solution_copy.wait()


def solution(mesh):
    counts = (mesh.shape["gx"], mesh.shape["gy"])

    def on_device(base_cond, base_mass, fine_residual, point_index, gen_vector, z_offset):
        planes, width_x, width_y = base_mass.shape
        assert (planes, width_x, width_y) == (4, 8, LANES)
        tiles = 4 * FIELDS
        widths = (width_x, width_y)
        row_shape = (tiles, 8, LANES)
        own_wide = (2 * tiles, 8, LANES)
        moved = (own_wide, (2,) + row_shape, (4, 3, 8, LANES), (8, ROWS, LANES))
        whole = pl.BlockSpec(memory_space=pltpu.HBM)
        between = pl.pallas_call(
            functools.partial(exchange, counts, widths),
            out_shape=tuple(jax.ShapeDtypeStruct(shape, jnp.float32) for shape in moved),
            in_specs=[whole] * 6,
            out_specs=[whole] * 4,
            scratch_shapes=[
                pltpu.VMEM((3, planes, width_x, width_y), jnp.float32),
                pltpu.VMEM((planes, width_x, width_y), jnp.float32),
                pltpu.VMEM((planes, width_x, width_y), jnp.float32),
                pltpu.SMEM((1, 1), jnp.int32),
                pltpu.SMEM((MODES,), jnp.int32),
                pltpu.SMEM((1, 1), jnp.int32),
                pltpu.VMEM(row_shape, jnp.float32),
                pltpu.VMEM((3, 8, LANES), jnp.float32),
                pltpu.VMEM((2, 3, 8, LANES), jnp.float32),
                pltpu.VMEM(own_wide, jnp.float32),
                pltpu.VMEM((8, ROWS, LANES), jnp.float32),
                pltpu.SemaphoreType.DMA((6,)),
                pltpu.SemaphoreType.DMA((8,)),
                pltpu.SemaphoreType.DMA((8,)),
                pltpu.SemaphoreType.DMA((2,)),
            ],
            compiler_params=pltpu.CompilerParams(
                collective_id=0, has_side_effects=True, vmem_limit_bytes=VMEM_GRANT
            ),
            name="exchange",
        )(
            base_cond, base_mass, fine_residual,
            point_index.reshape(1, 1), gen_vector, z_offset.reshape(1, 1),
        )
        out_planes, out_x, out_y = planes // 2, width_x // 2, width_y // 2
        stencil_shape, solution_shape = (27, out_planes, out_x, out_y), (out_planes, out_x, out_y)
        return pl.pallas_call(
            functools.partial(setup, counts, widths),
            out_shape=(
                jax.ShapeDtypeStruct(stencil_shape, jnp.float32),
                jax.ShapeDtypeStruct(solution_shape, jnp.float32),
            ),
            in_specs=[whole] * 4,
            out_specs=[whole] * 2,
            scratch_shapes=[pltpu.VMEM(shape, jnp.float32) for shape in moved[1:]]
            + [
                pltpu.VMEM((2 * tiles, ROWS, LANES), jnp.float32),
                pltpu.VMEM((28, 8, LANES), jnp.float32),
                pltpu.VMEM(stencil_shape, jnp.float32),
                pltpu.VMEM(solution_shape, jnp.float32),
                pltpu.SemaphoreType.DMA((4,)),
                pltpu.SemaphoreType.DMA((2,)),
            ],
            compiler_params=pltpu.CompilerParams(vmem_limit_bytes=VMEM_GRANT),
            name="setup",
        )(*between)

    return jax.shard_map(
        on_device,
        mesh=mesh,
        in_specs=(
            P(None, None, "gx", "gy"),
            P(None, "gx", "gy"),
            P("parts", "gx", "gy"),
            P("parts"),
            P(),
            P(),
        ),
        out_specs=(P(None, "parts", "gx", "gy"), P("parts", "gx", "gy")),
        check_vma=False,
    )
```

```python
import functools
import itertools
import math

import jax
import jax.numpy as jnp
from jax import lax
from jax.experimental import pallas as pl
from jax.experimental.pallas import tpu as pltpu
from jax.sharding import PartitionSpec as P

MESH = pl.DeviceIdType.MESH
NZG = 512
QMCN = 1048576
SWEEPS = 4
OMEGA = 0.6
MODES = 32
HALO = 4
CLASSES = list(itertools.product((0, 1), repeat=3))
FIELDS = 5
AXIS_FIELD = (2, 0, 1)
CORNERS = [(1, 1), (1, -1), (-1, 1), (-1, -1)]
BESIDE = [(0, 1), (0, -1)]
DIRECTIONS = [(-1, 1), (-1, -1)] + BESIDE + [(-1, 0), (1, 1), (1, -1), (1, 0)]
STRIP = 60
ROWS = 24
LANES = 128
VMEM_GRANT = 60 * 1024 * 1024


def cos_turns(turns):
    rest = 0.25 - jnp.abs(turns - jnp.round(turns))
    angle = rest * (2.0 * math.pi)
    square = angle * angle
    series = 1.0 / 6227020800.0
    for term in (-1.0 / 39916800.0, 1.0 / 362880.0, -1.0 / 5040.0, 1.0 / 120.0, -1.0 / 6.0, 1.0):
        series = series * square + term
    return series * angle


def shift(value, axis, step):
    if axis == 2:
        return pltpu.roll(value, (-step) % LANES, 1)
    return pltpu.roll(value, (-step * (1, 2)[axis]) % ROWS, 0)


def lanes_of(value, index):
    return jnp.take_along_axis(value, index, axis=1, mode="promise_in_bounds")


def flip(cls, axis):
    return tuple(1 - p if a == axis else p for a, p in enumerate(cls))


def split_lanes(tile, index):
    return lanes_of(tile, index)


def halves_of(value):
    high = value.astype(jnp.bfloat16)
    return high, (value - high.astype(jnp.float32)).astype(jnp.bfloat16)


def field_roots(scalars, x_first, y_first, nx_total, ny_total):
    half = MODES // 2
    point_ref, gen_ref, zoff_ref = scalars
    point = point_ref[0, 0]
    lane = lax.broadcasted_iota(jnp.int32, (1, 2 * MODES), 1)
    mode = (lane & (half - 1)) + jnp.where(lane < MODES, 0, half)
    shifts = jnp.zeros((1, 2 * MODES), jnp.int32)
    for k in range(MODES):
        shifts = jnp.where(mode == k, (point * gen_ref[k]) & (QMCN - 1), shifts)
    modef = mode.astype(jnp.float32)
    amplitude = (shifts.astype(jnp.float32) / QMCN - 0.5) * (1.2 / (1.0 + 0.5 * modef))
    freq_z = modef - 5.0 * jnp.floor((modef + 0.5) * 0.2)
    freq_x = (1 + (mode & 3)).astype(jnp.float32)
    phase = modef * (0.7 / (2.0 * math.pi)) - jnp.where((lane & half) == 0, 0.0, 0.25)
    row = lax.broadcasted_iota(jnp.int32, (ROWS, 1), 0)
    z_row = (zoff_ref[0, 0] + 2 * (row & 1)).astype(jnp.float32) + 0.5
    x_row = (x_first + 2 * ((row >> 1) - HALO)).astype(jnp.float32) + 0.5
    left = []
    for pz, px in itertools.product((0, 1), repeat=2):
        turns = (z_row + pz) * (freq_z / (2.0 * NZG)) + (x_row + px) * (freq_x / (2.0 * nx_total))
        left.append(amplitude * cos_turns(turns + phase))
    left = jnp.concatenate(left, axis=0)
    left = left[:, :MODES] + left[:, MODES:]
    mode_row = lax.broadcasted_iota(jnp.int32, (MODES, 1), 0)
    freq_y = (1 + ((mode_row >> 2) & 3)).astype(jnp.float32)
    quarter = jnp.where(mode_row < half, 0.0, 0.25)
    place = lax.broadcasted_iota(jnp.int32, (1, LANES), 1)
    coarse = jnp.where(place < LANES // 2 + HALO, place, place - LANES)
    right = []
    for py in (0, 1):
        y_place = (y_first + 2 * coarse + py).astype(jnp.float32) + 0.5
        right.append(cos_turns(freq_y * (y_place / (2.0 * ny_total)) + quarter))
    right = jnp.concatenate(right, axis=1)
    left_high, left_low = halves_of(left)
    right_high, right_low = halves_of(right)
    logs = jnp.dot(
        jnp.concatenate([left_high, left_high, left_low], axis=1),
        jnp.concatenate([right_high, right_low, right_high], axis=0),
        preferred_element_type=jnp.float32,
    )
    roots = jnp.exp(0.5 * logs)
    out = {}
    for n, (pz, px) in enumerate(itertools.product((0, 1), repeat=2)):
        for py in (0, 1):
            out[pz, px, py] = roots[n * ROWS:(n + 1) * ROWS, py * LANES:(py + 1) * LANES]
    return out


def coefficients(base, roots, x_first, y_first, nx_total, ny_total):
    row = lax.broadcasted_iota(jnp.int32, (ROWS, LANES), 0)
    place = lax.broadcasted_iota(jnp.int32, (ROWS, LANES), 1)
    x_even = x_first + 2 * ((row >> 1) - HALO)
    half = LANES // 2
    y_even = y_first + 2 * jnp.where(place < half + HALO, place, place - LANES)
    inside = (x_even >= 0) & (x_even < nx_total) & (y_even >= 0) & (y_even < ny_total)
    inside = inside & ((place < half + HALO) | (place >= LANES - HALO))
    inside = inside & (row < ROWS - 2)
    closed = (
        inside & ((row & 1) == 0),
        inside & (x_even + 2 < nx_total),
        inside & (y_even + 2 < ny_total),
    )
    cond, mass, residual = {}, {}, {}
    for cls in CLASSES:
        for axis in range(3):
            other = roots[flip(cls, axis)]
            if cls[axis]:
                other = shift(other, axis, 1)
            value = base(AXIS_FIELD[axis], cls) * roots[cls] * other
            cond[axis, cls] = jnp.where(closed[axis] if cls[axis] else inside, value, 0.0)
        mass[cls] = jnp.where(inside, base(3, cls) * (roots[cls] * roots[cls]), 1.0)
        residual[cls] = jnp.where(inside, base(4, cls), 0.0)
    return cond, mass, residual


def galerkin(cond, mass, residual):
    low = {}
    for cls in CLASSES:
        for axis in range(3):
            own = cond[axis, flip(cls, axis)]
            low[axis, cls] = own if cls[axis] else shift(own, axis, -1)

    weight = {((0, 0, 0), (0, 0, 0)): None}
    for cls in sorted(CLASSES, key=sum)[1:]:
        odd = [a for a in range(3) if cls[a]]
        total = mass[cls]
        for a in odd:
            total = total + (low[a, cls] + cond[a, cls])
        recip = 1.0 / total
        for corner in itertools.product(*[(0, 1) if p else (0,) for p in cls]):
            summed = None
            for a in odd:
                face = cond[a, cls] if corner[a] else low[a, cls]
                part = weight[flip(cls, a), tuple(0 if b == a else s for b, s in enumerate(corner))]
                if part is None:
                    term = face
                else:
                    term = face * (shift(part, a, 1) if corner[a] else part)
                summed = term if summed is None else summed + term
            weight[cls, corner] = recip * summed

    def wanted(offset):
        return offset >= (0, 0, 0)

    parts = {}

    def add(corner, offset, value):
        slot = parts.setdefault(offset, {})
        slot[corner] = slot[corner] + value if corner in slot else value

    for cls in sorted(CLASSES, key=sum)[:-1]:
        even = [a for a in range(3) if not cls[a]]
        pairs = None
        for a in even:
            pair = low[a, cls] + cond[a, cls]
            pairs = pair if pairs is None else pairs + pair
        if sum(cls) == 0:
            pairs = pairs + mass[cls]
        corners = list(itertools.product(*[(0, 1) if p else (0,) for p in cls]))
        applied = {}
        for corner in corners:
            own = weight[cls, corner]
            centre = pairs if own is None else pairs * own
            for a in even:
                up = flip(cls, a)
                high = tuple(1 if b == a else s for b, s in enumerate(corner))
                to_low = cond[a, up] * weight[up, corner]
                to_high = cond[a, up] * weight[up, high]
                centre = centre - shift(to_high, a, -1) - cond[a, cls] * weight[up, corner]
                below = tuple(-1 if b == a else s for b, s in enumerate(corner))
                applied[below] = -shift(to_low, a, -1)
                applied[high] = -(cond[a, cls] * weight[up, high])
            applied[corner] = centre
        for corner in corners:
            own = weight[cls, corner]
            for target, value in applied.items():
                offset = tuple(t - s for t, s in zip(target, corner))
                if wanted(offset):
                    add(corner, offset, value if own is None else own * value)

    def collect(slot):
        for axis in range(3):
            merged = {}
            for corner, value in slot.items():
                if corner[axis] == 0:
                    merged[corner] = merged[corner] + value if corner in merged else value
            for corner, value in slot.items():
                if corner[axis] == 1:
                    key = tuple(0 if b == axis else s for b, s in enumerate(corner))
                    moved = shift(value, axis, -1)
                    merged[key] = merged[key] + moved if key in merged else moved
            slot = merged
        return slot[0, 0, 0]

    stencil = {offset: collect(slot) for offset, slot in parts.items()}
    for offset in list(stencil):
        if offset != (0, 0, 0):
            value = stencil[offset]
            for axis, step in enumerate(offset):
                if step:
                    value = shift(value, axis, -step)
            stencil[tuple(-o for o in offset)] = value

    slot = {(0, 0, 0): residual[0, 0, 0]}
    for (cls, corner), own in weight.items():
        if own is not None:
            term = own * residual[cls]
            slot[corner] = slot[corner] + term if corner in slot else term
    return stencil, collect(slot)


def sweep_all(stencil, rhs):
    row = lax.broadcasted_iota(jnp.int32, (ROWS, LANES), 0)
    place = lax.broadcasted_iota(jnp.int32, (ROWS, LANES), 1)
    reach = HALO - 1
    valid = (row >= 2) & (row < ROWS - 2)
    valid = valid & ((place < LANES // 2 + reach) | (place >= LANES - reach))
    scale = jnp.where(valid, OMEGA / jnp.where(valid, stencil[0, 0, 0], 1.0), 0.0)
    values = rhs * scale
    for _ in range(SWEEPS - 1):
        rest = rhs
        for dz in (-1, 0, 1):
            in_z = shift(values, 0, dz) if dz else values
            for dx in (-1, 0, 1):
                in_x = shift(in_z, 1, dx) if dx else in_z
                for dy in (-1, 0, 1):
                    in_y = shift(in_x, 2, dy) if dy else in_x
                    rest = rest - stencil[dz, dx, dy] * in_y
        values = values + rest * scale
    return values


def place_of(counts, widths):
    gx, gy = lax.axis_index("gx"), lax.axis_index("gy")
    (nx_devices, ny_devices), (width_x, width_y) = counts, widths
    return gx * width_x, gy * width_y, nx_devices * width_x, ny_devices * width_y


def exchange(
    counts, widths, cond_hbm, mass_hbm, res_hbm, point_hbm, gen_hbm, zoff_hbm,
    wide_hbm, side, strips, roots_hbm,
    cond_in, mass_in, res_in, point_ref, gen_ref, zoff_ref, own, strip, beside, wide, roots_out,
    in_sem, send_sem, recv_sem, out_sem,
):
    parts_at = lax.axis_index("parts")
    gx, gy = lax.axis_index("gx"), lax.axis_index("gy")
    nx_devices, ny_devices = counts

    def present(sx, sy):
        conditions = []
        if sx:
            conditions.append(gx > 0 if sx < 0 else gx < nx_devices - 1)
        if sy:
            conditions.append(gy > 0 if sy < 0 else gy < ny_devices - 1)
        return functools.reduce(jnp.logical_and, conditions)

    barrier = pltpu.get_barrier_semaphore()
    neighbours = 0
    for sx, sy in DIRECTIONS:
        there = present(sx, sy)
        neighbours = neighbours + there.astype(jnp.int32)

        @pl.when(there)
        def _():
            pl.semaphore_signal(
                barrier, inc=1, device_id=(parts_at, gx + sx, gy + sy), device_id_type=MESH
            )

    loads = [
        pltpu.make_async_copy(source, target, in_sem.at[n])
        for n, (source, target) in enumerate(
            (
                (cond_hbm, cond_in),
                (mass_hbm, mass_in),
                (res_hbm, res_in),
                (point_hbm, point_ref),
                (gen_hbm, gen_ref),
                (zoff_hbm, zoff_ref),
            )
        )
    ]
    for load in loads:
        load.start()
    for load in loads:
        load.wait()

    lane = lax.broadcasted_iota(jnp.int32, (8, LANES), 1)
    half = LANES // 2
    to_halves = jnp.where(lane < half, 2 * lane, 2 * lane - (LANES - 1))
    first, last = lane & 7, (lane - STRIP) & 7
    to_strip = jnp.where(
        lane < STRIP,
        first + jnp.where(first < 4, 0, half - 4),
        last + jnp.where(last < 4, half - 4, LANES - 8),
    )
    slot = jnp.where(lane < STRIP, lane >> 3, (lane - STRIP) >> 3)
    packs = [None] * 3
    for field in range(FIELDS):
        for pz in (0, 1):
            for px in (0, 1):
                t = 4 * field + 2 * pz + px
                for zc in (0, 1):
                    plane = 2 * zc + pz
                    if field < 3:
                        piece = cond_in[field, plane, pl.ds(px, 4, stride=2), :]
                    else:
                        source = mass_in if field == 3 else res_in
                        piece = source[plane, pl.ds(px, 4, stride=2), :]
                    own[t, pl.ds(zc, 4, stride=2), :] = piece
                halves = lanes_of(own[t], to_halves)
                own[t] = halves
                word, place = divmod(t, 7)
                packed = lanes_of(halves, to_strip)
                packs[word] = jnp.where(slot == place, packed, packs[word]) if place else packed
    for word in range(3):
        strip[word] = packs[word]

    pl.semaphore_wait(barrier, neighbours)

    def copy_to(n):
        sx, sy = DIRECTIONS[n]
        if sy == 0:
            source, target = own, side.at[0 if sx == 1 else 1]
            if sx == -1:
                source, target = source.at[:, pl.ds(0, 6)], target.at[:, pl.ds(0, 6)]
        else:
            source = strip
            target = strips.at[CORNERS.index((sx, sy))] if sx else beside.at[0 if sy == 1 else 1]
        return pltpu.make_async_remote_copy(
            src_ref=source,
            dst_ref=target,
            send_sem=send_sem.at[n],
            recv_sem=recv_sem.at[n],
            device_id=(parts_at, gx + sx, gy + sy),
            device_id_type=MESH,
        )

    for n, (sx, sy) in enumerate(DIRECTIONS):
        @pl.when(present(sx, sy))
        def _():
            copy_to(n).start()

    roots = field_roots((point_ref, gen_ref, zoff_ref), *place_of(counts, widths))
    for n, cls in enumerate(CLASSES):
        roots_out[n] = roots[cls]
    roots_copy = pltpu.make_async_copy(roots_out, roots_hbm, out_sem.at[1])
    roots_copy.start()

    def finish(directions):
        for direction in directions:
            n = DIRECTIONS.index(direction)

            @pl.when(present(-direction[0], -direction[1]))
            def _():
                copy_to(n).wait_recv()

            @pl.when(present(*direction))
            def _():
                copy_to(n).wait_send()

    finish(BESIDE)
    assemble(own, beside.at[0], beside.at[1], wide, 0)
    wide_copy = pltpu.make_async_copy(wide, wide_hbm, out_sem.at[0])
    wide_copy.start()
    finish([direction for direction in DIRECTIONS if direction not in BESIDE])
    roots_copy.wait()
    wide_copy.wait()


def assemble(tiles, from_low, from_high, wide, first_row):
    lane = lax.broadcasted_iota(jnp.int32, (8, LANES), 1)
    half = LANES // 2
    merged = [jnp.where(lane < STRIP, from_high[w], from_low[w]) for w in range(3)]
    for t in range(4 * FIELDS):
        tile = tiles[t]
        word, place = divmod(t, 7)
        for py in (0, 1):
            edge = pltpu.roll(merged[word], half - 8 * place - 4 * py, 1)
            middle = pltpu.roll(tile, half, 1) if py else tile
            wide[2 * t + py, pl.ds(first_row, 8), :] = jnp.where(lane < half, middle, edge)


def setup(
    counts, widths, wide_hbm, side_hbm, strips_hbm, roots_hbm, stencil_hbm, solution_hbm,
    side, strips, roots_ref, wide, rows_out, stencil_out, solution_out, in_sem, sem,
):
    loads = [
        pltpu.make_async_copy(source, target, in_sem.at[n])
        for n, (source, target) in enumerate(
            (
                (side_hbm, side),
                (strips_hbm, strips),
                (wide_hbm, wide.at[:, pl.ds(8, 8)]),
                (roots_hbm, roots_ref),
            )
        )
    ]
    for load in loads:
        load.start()
    for load in loads:
        load.wait()
    for block, sx in ((0, 1), (2, -1)):
        from_low, from_high = (strips.at[CORNERS.index((sx, sy))] for sy in (1, -1))
        assemble(side.at[block // 2], from_low, from_high, wide, 8 * block)

    def base(field, cls):
        return wide[8 * field + 4 * cls[0] + 2 * cls[1] + cls[2]]

    half = LANES // 2
    roots = {cls: roots_ref[n] for n, cls in enumerate(CLASSES)}
    cond, mass, residual = coefficients(base, roots, *place_of(counts, widths))
    stencil, rhs = galerkin(cond, mass, residual)
    for (dz, dx, dy), value in stencil.items():
        rows_out[9 * (dz + 1) + 3 * (dx + 1) + (dy + 1)] = value[8:16]
    for zc in (0, 1):
        for d in range(27):
            stencil_out[d, zc] = rows_out[d, pl.ds(zc, 4, stride=2), :][:, :half]
    stencil_copy = pltpu.make_async_copy(stencil_out, stencil_hbm, sem.at[0])
    stencil_copy.start()
    rows_out[27] = sweep_all(stencil, rhs)[8:16]
    for zc in (0, 1):
        solution_out[zc] = rows_out[27, pl.ds(zc, 4, stride=2), :][:, :half]
    solution_copy = pltpu.make_async_copy(solution_out, solution_hbm, sem.at[1])
    solution_copy.start()
    stencil_copy.wait()
    solution_copy.wait()


def solution(mesh):
    counts = (mesh.shape["gx"], mesh.shape["gy"])

    def on_device(base_cond, base_mass, fine_residual, point_index, gen_vector, z_offset):
        planes, width_x, width_y = base_mass.shape
        assert (planes, width_x, width_y) == (4, 8, LANES)
        tiles = 4 * FIELDS
        widths = (width_x, width_y)
        row_shape = (tiles, 8, LANES)
        own_wide = (2 * tiles, 8, LANES)
        moved = (own_wide, (2,) + row_shape, (4, 3, 8, LANES), (8, ROWS, LANES))
        whole = pl.BlockSpec(memory_space=pltpu.HBM)
        between = pl.pallas_call(
            functools.partial(exchange, counts, widths),
            out_shape=tuple(jax.ShapeDtypeStruct(shape, jnp.float32) for shape in moved),
            in_specs=[whole] * 6,
            out_specs=[whole] * 4,
            scratch_shapes=[
                pltpu.VMEM((3, planes, width_x, width_y), jnp.float32),
                pltpu.VMEM((planes, width_x, width_y), jnp.float32),
                pltpu.VMEM((planes, width_x, width_y), jnp.float32),
                pltpu.SMEM((1, 1), jnp.int32),
                pltpu.SMEM((MODES,), jnp.int32),
                pltpu.SMEM((1, 1), jnp.int32),
                pltpu.VMEM(row_shape, jnp.float32),
                pltpu.VMEM((3, 8, LANES), jnp.float32),
                pltpu.VMEM((2, 3, 8, LANES), jnp.float32),
                pltpu.VMEM(own_wide, jnp.float32),
                pltpu.VMEM((8, ROWS, LANES), jnp.float32),
                pltpu.SemaphoreType.DMA((6,)),
                pltpu.SemaphoreType.DMA((8,)),
                pltpu.SemaphoreType.DMA((8,)),
                pltpu.SemaphoreType.DMA((2,)),
            ],
            compiler_params=pltpu.CompilerParams(
                collective_id=0, has_side_effects=True, vmem_limit_bytes=VMEM_GRANT
            ),
            name="exchange",
        )(
            base_cond, base_mass, fine_residual,
            point_index.reshape(1, 1), gen_vector, z_offset.reshape(1, 1),
        )
        out_planes, out_x, out_y = planes // 2, width_x // 2, width_y // 2
        stencil_shape, solution_shape = (27, out_planes, out_x, out_y), (out_planes, out_x, out_y)
        return pl.pallas_call(
            functools.partial(setup, counts, widths),
            out_shape=(
                jax.ShapeDtypeStruct(stencil_shape, jnp.float32),
                jax.ShapeDtypeStruct(solution_shape, jnp.float32),
            ),
            in_specs=[whole] * 4,
            out_specs=[whole] * 2,
            scratch_shapes=[pltpu.VMEM(shape, jnp.float32) for shape in moved[1:]]
            + [
                pltpu.VMEM((2 * tiles, ROWS, LANES), jnp.float32),
                pltpu.VMEM((28, 8, LANES), jnp.float32),
                pltpu.VMEM(stencil_shape, jnp.float32),
                pltpu.VMEM(solution_shape, jnp.float32),
                pltpu.SemaphoreType.DMA((4,)),
                pltpu.SemaphoreType.DMA((2,)),
            ],
            compiler_params=pltpu.CompilerParams(vmem_limit_bytes=VMEM_GRANT),
            name="setup",
        )(*between)

    return jax.shard_map(
        on_device,
        mesh=mesh,
        in_specs=(
            P(None, None, "gx", "gy"),
            P(None, "gx", "gy"),
            P("parts", "gx", "gy"),
            P("parts"),
            P(),
            P(),
        ),
        out_specs=(P(None, "parts", "gx", "gy"), P("parts", "gx", "gy")),
        check_vma=False,
    )
```

```python
import functools
import itertools
import math

import jax
import jax.numpy as jnp
from jax import lax
from jax.experimental import pallas as pl
from jax.experimental.pallas import tpu as pltpu
from jax.sharding import PartitionSpec as P

MESH = pl.DeviceIdType.MESH
NZG = 512
QMCN = 1048576
SWEEPS = 4
OMEGA = 0.6
MODES = 32
HALO = 4
CLASSES = list(itertools.product((0, 1), repeat=3))
FIELDS = 5
AXIS_FIELD = (2, 0, 1)
CORNERS = [(1, 1), (1, -1), (-1, 1), (-1, -1)]
BESIDE = [(0, 1), (0, -1)]
STRIPS = CORNERS + BESIDE
DIRECTIONS = [(-1, 1), (-1, -1)] + BESIDE + [(-1, 0), (1, 1), (1, -1), (1, 0)]
STRIP = 60
ROWS = 24
LANES = 128
VMEM_GRANT = 60 * 1024 * 1024


def cos_turns(turns):
    rest = 0.25 - jnp.abs(turns - jnp.round(turns))
    angle = rest * (2.0 * math.pi)
    square = angle * angle
    series = 1.0 / 6227020800.0
    for term in (-1.0 / 39916800.0, 1.0 / 362880.0, -1.0 / 5040.0, 1.0 / 120.0, -1.0 / 6.0, 1.0):
        series = series * square + term
    return series * angle


def shift(value, axis, step):
    if axis == 2:
        return pltpu.roll(value, (-step) % LANES, 1)
    return pltpu.roll(value, (-step * (1, 2)[axis]) % ROWS, 0)


def lanes_of(value, index):
    return jnp.take_along_axis(value, index, axis=1, mode="promise_in_bounds")


def flip(cls, axis):
    return tuple(1 - p if a == axis else p for a, p in enumerate(cls))


def split_lanes(tile, index):
    return lanes_of(tile, index)


def halves_of(value):
    high = value.astype(jnp.bfloat16)
    return high, (value - high.astype(jnp.float32)).astype(jnp.bfloat16)


def field_roots(scalars, x_first, y_first, nx_total, ny_total):
    half = MODES // 2
    point_ref, gen_ref, zoff_ref = scalars
    point = point_ref[0, 0]
    lane = lax.broadcasted_iota(jnp.int32, (1, 2 * MODES), 1)
    mode = (lane & (half - 1)) + jnp.where(lane < MODES, 0, half)
    shifts = jnp.zeros((1, 2 * MODES), jnp.int32)
    for k in range(MODES):
        shifts = jnp.where(mode == k, (point * gen_ref[k]) & (QMCN - 1), shifts)
    modef = mode.astype(jnp.float32)
    amplitude = (shifts.astype(jnp.float32) / QMCN - 0.5) * (1.2 / (1.0 + 0.5 * modef))
    freq_z = modef - 5.0 * jnp.floor((modef + 0.5) * 0.2)
    freq_x = (1 + (mode & 3)).astype(jnp.float32)
    phase = modef * (0.7 / (2.0 * math.pi)) - jnp.where((lane & half) == 0, 0.0, 0.25)
    row = lax.broadcasted_iota(jnp.int32, (ROWS, 1), 0)
    z_row = (zoff_ref[0, 0] + 2 * (row & 1)).astype(jnp.float32) + 0.5
    x_row = (x_first + 2 * ((row >> 1) - HALO)).astype(jnp.float32) + 0.5
    left = []
    for pz, px in itertools.product((0, 1), repeat=2):
        turns = (z_row + pz) * (freq_z / (2.0 * NZG)) + (x_row + px) * (freq_x / (2.0 * nx_total))
        left.append(amplitude * cos_turns(turns + phase))
    left = jnp.concatenate(left, axis=0)
    left = left[:, :MODES] + left[:, MODES:]
    mode_row = lax.broadcasted_iota(jnp.int32, (MODES, 1), 0)
    freq_y = (1 + ((mode_row >> 2) & 3)).astype(jnp.float32)
    quarter = jnp.where(mode_row < half, 0.0, 0.25)
    place = lax.broadcasted_iota(jnp.int32, (1, LANES), 1)
    coarse = jnp.where(place < LANES // 2 + HALO, place, place - LANES)
    right = []
    for py in (0, 1):
        y_place = (y_first + 2 * coarse + py).astype(jnp.float32) + 0.5
        right.append(cos_turns(freq_y * (y_place / (2.0 * ny_total)) + quarter))
    right = jnp.concatenate(right, axis=1)
    left_high, left_low = halves_of(left)
    right_high, right_low = halves_of(right)
    logs = jnp.dot(
        jnp.concatenate([left_high, left_high, left_low], axis=1),
        jnp.concatenate([right_high, right_low, right_high], axis=0),
        preferred_element_type=jnp.float32,
    )
    roots = jnp.exp(0.5 * logs)
    out = {}
    for n, (pz, px) in enumerate(itertools.product((0, 1), repeat=2)):
        for py in (0, 1):
            out[pz, px, py] = roots[n * ROWS:(n + 1) * ROWS, py * LANES:(py + 1) * LANES]
    return out


def coefficients(base, roots, x_first, y_first, nx_total, ny_total):
    row = lax.broadcasted_iota(jnp.int32, (ROWS, LANES), 0)
    place = lax.broadcasted_iota(jnp.int32, (ROWS, LANES), 1)
    x_even = x_first + 2 * ((row >> 1) - HALO)
    half = LANES // 2
    y_even = y_first + 2 * jnp.where(place < half + HALO, place, place - LANES)
    inside = (x_even >= 0) & (x_even < nx_total) & (y_even >= 0) & (y_even < ny_total)
    inside = inside & ((place < half + HALO) | (place >= LANES - HALO))
    inside = inside & (row < ROWS - 2)
    closed = (
        inside & ((row & 1) == 0),
        inside & (x_even + 2 < nx_total),
        inside & (y_even + 2 < ny_total),
    )
    cond, mass, residual = {}, {}, {}
    for cls in CLASSES:
        for axis in range(3):
            other = roots[flip(cls, axis)]
            if cls[axis]:
                other = shift(other, axis, 1)
            value = base(AXIS_FIELD[axis], cls) * roots[cls] * other
            cond[axis, cls] = jnp.where(closed[axis] if cls[axis] else inside, value, 0.0)
        mass[cls] = jnp.where(inside, base(3, cls) * (roots[cls] * roots[cls]), 1.0)
        residual[cls] = jnp.where(inside, base(4, cls), 0.0)
    return cond, mass, residual


def galerkin(cond, mass, residual):
    low = {}
    for cls in CLASSES:
        for axis in range(3):
            own = cond[axis, flip(cls, axis)]
            low[axis, cls] = own if cls[axis] else shift(own, axis, -1)

    weight = {((0, 0, 0), (0, 0, 0)): None}
    for cls in sorted(CLASSES, key=sum)[1:]:
        odd = [a for a in range(3) if cls[a]]
        total = mass[cls]
        for a in odd:
            total = total + (low[a, cls] + cond[a, cls])
        recip = 1.0 / total
        for corner in itertools.product(*[(0, 1) if p else (0,) for p in cls]):
            summed = None
            for a in odd:
                face = cond[a, cls] if corner[a] else low[a, cls]
                part = weight[flip(cls, a), tuple(0 if b == a else s for b, s in enumerate(corner))]
                if part is None:
                    term = face
                else:
                    term = face * (shift(part, a, 1) if corner[a] else part)
                summed = term if summed is None else summed + term
            weight[cls, corner] = recip * summed

    def wanted(offset):
        return offset >= (0, 0, 0)

    parts = {}

    def add(corner, offset, value):
        slot = parts.setdefault(offset, {})
        slot[corner] = slot[corner] + value if corner in slot else value

    for cls in sorted(CLASSES, key=sum)[:-1]:
        even = [a for a in range(3) if not cls[a]]
        pairs = None
        for a in even:
            pair = low[a, cls] + cond[a, cls]
            pairs = pair if pairs is None else pairs + pair
        if sum(cls) == 0:
            pairs = pairs + mass[cls]
        corners = list(itertools.product(*[(0, 1) if p else (0,) for p in cls]))
        applied = {}
        for corner in corners:
            own = weight[cls, corner]
            centre = pairs if own is None else pairs * own
            for a in even:
                up = flip(cls, a)
                high = tuple(1 if b == a else s for b, s in enumerate(corner))
                to_low = cond[a, up] * weight[up, corner]
                to_high = cond[a, up] * weight[up, high]
                centre = centre - shift(to_high, a, -1) - cond[a, cls] * weight[up, corner]
                below = tuple(-1 if b == a else s for b, s in enumerate(corner))
                applied[below] = -shift(to_low, a, -1)
                applied[high] = -(cond[a, cls] * weight[up, high])
            applied[corner] = centre
        for corner in corners:
            own = weight[cls, corner]
            for target, value in applied.items():
                offset = tuple(t - s for t, s in zip(target, corner))
                if wanted(offset):
                    add(corner, offset, value if own is None else own * value)

    def collect(slot):
        for axis in range(3):
            merged = {}
            for corner, value in slot.items():
                if corner[axis] == 0:
                    merged[corner] = merged[corner] + value if corner in merged else value
            for corner, value in slot.items():
                if corner[axis] == 1:
                    key = tuple(0 if b == axis else s for b, s in enumerate(corner))
                    moved = shift(value, axis, -1)
                    merged[key] = merged[key] + moved if key in merged else moved
            slot = merged
        return slot[0, 0, 0]

    stencil = {offset: collect(slot) for offset, slot in parts.items()}
    for offset in list(stencil):
        if offset != (0, 0, 0):
            value = stencil[offset]
            for axis, step in enumerate(offset):
                if step:
                    value = shift(value, axis, -step)
            stencil[tuple(-o for o in offset)] = value

    slot = {(0, 0, 0): residual[0, 0, 0]}
    for (cls, corner), own in weight.items():
        if own is not None:
            term = own * residual[cls]
            slot[corner] = slot[corner] + term if corner in slot else term
    return stencil, collect(slot)


def sweep_all(stencil, rhs):
    row = lax.broadcasted_iota(jnp.int32, (ROWS, LANES), 0)
    place = lax.broadcasted_iota(jnp.int32, (ROWS, LANES), 1)
    reach = HALO - 1
    valid = (row >= 2) & (row < ROWS - 2)
    valid = valid & ((place < LANES // 2 + reach) | (place >= LANES - reach))
    scale = jnp.where(valid, OMEGA / jnp.where(valid, stencil[0, 0, 0], 1.0), 0.0)
    values = rhs * scale
    for _ in range(SWEEPS - 1):
        rest = rhs
        for dz in (-1, 0, 1):
            in_z = shift(values, 0, dz) if dz else values
            for dx in (-1, 0, 1):
                in_x = shift(in_z, 1, dx) if dx else in_z
                for dy in (-1, 0, 1):
                    in_y = shift(in_x, 2, dy) if dy else in_x
                    rest = rest - stencil[dz, dx, dy] * in_y
        values = values + rest * scale
    return values


def place_of(counts, widths):
    gx, gy = lax.axis_index("gx"), lax.axis_index("gy")
    (nx_devices, ny_devices), (width_x, width_y) = counts, widths
    return gx * width_x, gy * width_y, nx_devices * width_x, ny_devices * width_y


def exchange(
    counts, widths, cond_hbm, mass_hbm, res_hbm, point_hbm, gen_hbm, zoff_hbm,
    own_hbm, side, strips, roots_hbm,
    cond_in, mass_in, res_in, point_ref, gen_ref, zoff_ref, own, strip, roots_out,
    in_sem, send_sem, recv_sem, out_sem,
):
    parts_at = lax.axis_index("parts")
    gx, gy = lax.axis_index("gx"), lax.axis_index("gy")
    nx_devices, ny_devices = counts

    def present(sx, sy):
        conditions = []
        if sx:
            conditions.append(gx > 0 if sx < 0 else gx < nx_devices - 1)
        if sy:
            conditions.append(gy > 0 if sy < 0 else gy < ny_devices - 1)
        return functools.reduce(jnp.logical_and, conditions)

    barrier = pltpu.get_barrier_semaphore()
    neighbours = 0
    for sx, sy in DIRECTIONS:
        there = present(sx, sy)
        neighbours = neighbours + there.astype(jnp.int32)

        @pl.when(there)
        def _():
            pl.semaphore_signal(
                barrier, inc=1, device_id=(parts_at, gx + sx, gy + sy), device_id_type=MESH
            )

    loads = [
        pltpu.make_async_copy(source, target, in_sem.at[n])
        for n, (source, target) in enumerate(
            (
                (cond_hbm, cond_in),
                (mass_hbm, mass_in),
                (res_hbm, res_in),
                (point_hbm, point_ref),
                (gen_hbm, gen_ref),
                (zoff_hbm, zoff_ref),
            )
        )
    ]
    for load in loads:
        load.start()
    for load in loads:
        load.wait()

    lane = lax.broadcasted_iota(jnp.int32, (8, LANES), 1)
    half = LANES // 2
    to_halves = jnp.where(lane < half, 2 * lane, 2 * lane - (LANES - 1))
    first, last = lane & 7, (lane - STRIP) & 7
    to_strip = jnp.where(
        lane < STRIP,
        first + jnp.where(first < 4, 0, half - 4),
        last + jnp.where(last < 4, half - 4, LANES - 8),
    )
    slot = jnp.where(lane < STRIP, lane >> 3, (lane - STRIP) >> 3)
    packs = [None] * 3
    for field in range(FIELDS):
        for pz in (0, 1):
            for px in (0, 1):
                t = 4 * field + 2 * pz + px
                for zc in (0, 1):
                    plane = 2 * zc + pz
                    if field < 3:
                        piece = cond_in[field, plane, pl.ds(px, 4, stride=2), :]
                    else:
                        source = mass_in if field == 3 else res_in
                        piece = source[plane, pl.ds(px, 4, stride=2), :]
                    own[t, pl.ds(zc, 4, stride=2), :] = piece
                halves = lanes_of(own[t], to_halves)
                own[t] = halves
                word, place = divmod(t, 7)
                packed = lanes_of(halves, to_strip)
                packs[word] = jnp.where(slot == place, packed, packs[word]) if place else packed
    for word in range(3):
        strip[word] = packs[word]

    pl.semaphore_wait(barrier, neighbours)

    def copy_to(n):
        sx, sy = DIRECTIONS[n]
        if sy == 0:
            source, target = own, side.at[0 if sx == 1 else 1]
            if sx == -1:
                source, target = source.at[:, pl.ds(0, 6)], target.at[:, pl.ds(0, 6)]
        else:
            source = strip
            target = strips.at[STRIPS.index((sx, sy))]
        return pltpu.make_async_remote_copy(
            src_ref=source,
            dst_ref=target,
            send_sem=send_sem.at[n],
            recv_sem=recv_sem.at[n],
            device_id=(parts_at, gx + sx, gy + sy),
            device_id_type=MESH,
        )

    for n, (sx, sy) in enumerate(DIRECTIONS):
        @pl.when(present(sx, sy))
        def _():
            copy_to(n).start()

    own_copy = pltpu.make_async_copy(own, own_hbm, out_sem.at[0])
    own_copy.start()
    roots = field_roots((point_ref, gen_ref, zoff_ref), *place_of(counts, widths))
    for n, cls in enumerate(CLASSES):
        roots_out[n] = roots[cls]
    roots_copy = pltpu.make_async_copy(roots_out, roots_hbm, out_sem.at[1])
    roots_copy.start()

    def finish(directions):
        for direction in directions:
            n = DIRECTIONS.index(direction)

            @pl.when(present(-direction[0], -direction[1]))
            def _():
                copy_to(n).wait_recv()

            @pl.when(present(*direction))
            def _():
                copy_to(n).wait_send()

    finish(DIRECTIONS)
    roots_copy.wait()
    own_copy.wait()


def assemble(tiles, from_low, from_high, wide, first_row):
    lane = lax.broadcasted_iota(jnp.int32, (8, LANES), 1)
    half = LANES // 2
    merged = [jnp.where(lane < STRIP, from_high[w], from_low[w]) for w in range(3)]
    for t in range(4 * FIELDS):
        tile = tiles[t]
        word, place = divmod(t, 7)
        for py in (0, 1):
            edge = pltpu.roll(merged[word], half - 8 * place - 4 * py, 1)
            middle = pltpu.roll(tile, half, 1) if py else tile
            wide[2 * t + py, pl.ds(first_row, 8), :] = jnp.where(lane < half, middle, edge)


def setup(
    counts, widths, own_hbm, side_hbm, strips_hbm, roots_hbm, stencil_hbm, solution_hbm,
    own, side, strips, roots_ref, wide, rows_out, stencil_out, solution_out, in_sem, sem,
):
    loads = [
        pltpu.make_async_copy(source, target, in_sem.at[n])
        for n, (source, target) in enumerate(
            (
                (side_hbm, side),
                (strips_hbm, strips),
                (own_hbm, own),
                (roots_hbm, roots_ref),
            )
        )
    ]
    for load in loads:
        load.start()
    for load in loads:
        load.wait()
    for block, (tiles, sx) in enumerate(((side.at[0], 1), (own, 0), (side.at[1], -1))):
        from_low, from_high = (strips.at[STRIPS.index((sx, sy))] for sy in (1, -1))
        assemble(tiles, from_low, from_high, wide, 8 * block)

    def base(field, cls):
        return wide[8 * field + 4 * cls[0] + 2 * cls[1] + cls[2]]

    half = LANES // 2
    roots = {cls: roots_ref[n] for n, cls in enumerate(CLASSES)}
    cond, mass, residual = coefficients(base, roots, *place_of(counts, widths))
    stencil, rhs = galerkin(cond, mass, residual)
    for (dz, dx, dy), value in stencil.items():
        rows_out[9 * (dz + 1) + 3 * (dx + 1) + (dy + 1)] = value[8:16]
    for zc in (0, 1):
        for d in range(27):
            stencil_out[d, zc] = rows_out[d, pl.ds(zc, 4, stride=2), :][:, :half]
    stencil_copy = pltpu.make_async_copy(stencil_out, stencil_hbm, sem.at[0])
    stencil_copy.start()
    rows_out[27] = sweep_all(stencil, rhs)[8:16]
    for zc in (0, 1):
        solution_out[zc] = rows_out[27, pl.ds(zc, 4, stride=2), :][:, :half]
    solution_copy = pltpu.make_async_copy(solution_out, solution_hbm, sem.at[1])
    solution_copy.start()
    stencil_copy.wait()
    solution_copy.wait()


def solution(mesh):
    counts = (mesh.shape["gx"], mesh.shape["gy"])

    def on_device(base_cond, base_mass, fine_residual, point_index, gen_vector, z_offset):
        planes, width_x, width_y = base_mass.shape
        assert (planes, width_x, width_y) == (4, 8, LANES)
        tiles = 4 * FIELDS
        widths = (width_x, width_y)
        row_shape = (tiles, 8, LANES)
        moved = (row_shape, (2,) + row_shape, (6, 3, 8, LANES), (8, ROWS, LANES))
        whole = pl.BlockSpec(memory_space=pltpu.HBM)
        between = pl.pallas_call(
            functools.partial(exchange, counts, widths),
            out_shape=tuple(jax.ShapeDtypeStruct(shape, jnp.float32) for shape in moved),
            in_specs=[whole] * 6,
            out_specs=[whole] * 4,
            scratch_shapes=[
                pltpu.VMEM((3, planes, width_x, width_y), jnp.float32),
                pltpu.VMEM((planes, width_x, width_y), jnp.float32),
                pltpu.VMEM((planes, width_x, width_y), jnp.float32),
                pltpu.SMEM((1, 1), jnp.int32),
                pltpu.SMEM((MODES,), jnp.int32),
                pltpu.SMEM((1, 1), jnp.int32),
                pltpu.VMEM(row_shape, jnp.float32),
                pltpu.VMEM((3, 8, LANES), jnp.float32),
                pltpu.VMEM((8, ROWS, LANES), jnp.float32),
                pltpu.SemaphoreType.DMA((6,)),
                pltpu.SemaphoreType.DMA((8,)),
                pltpu.SemaphoreType.DMA((8,)),
                pltpu.SemaphoreType.DMA((2,)),
            ],
            compiler_params=pltpu.CompilerParams(
                collective_id=0, has_side_effects=True, vmem_limit_bytes=VMEM_GRANT
            ),
            name="exchange",
        )(
            base_cond, base_mass, fine_residual,
            point_index.reshape(1, 1), gen_vector, z_offset.reshape(1, 1),
        )
        out_planes, out_x, out_y = planes // 2, width_x // 2, width_y // 2
        stencil_shape, solution_shape = (27, out_planes, out_x, out_y), (out_planes, out_x, out_y)
        return pl.pallas_call(
            functools.partial(setup, counts, widths),
            out_shape=(
                jax.ShapeDtypeStruct(stencil_shape, jnp.float32),
                jax.ShapeDtypeStruct(solution_shape, jnp.float32),
            ),
            in_specs=[whole] * 4,
            out_specs=[whole] * 2,
            scratch_shapes=[pltpu.VMEM(shape, jnp.float32) for shape in moved]
            + [
                pltpu.VMEM((2 * tiles, ROWS, LANES), jnp.float32),
                pltpu.VMEM((28, 8, LANES), jnp.float32),
                pltpu.VMEM(stencil_shape, jnp.float32),
                pltpu.VMEM(solution_shape, jnp.float32),
                pltpu.SemaphoreType.DMA((4,)),
                pltpu.SemaphoreType.DMA((2,)),
            ],
            compiler_params=pltpu.CompilerParams(vmem_limit_bytes=VMEM_GRANT),
            name="setup",
        )(*between)

    return jax.shard_map(
        on_device,
        mesh=mesh,
        in_specs=(
            P(None, None, "gx", "gy"),
            P(None, "gx", "gy"),
            P("parts", "gx", "gy"),
            P("parts"),
            P(),
            P(),
        ),
        out_specs=(P(None, "parts", "gx", "gy"), P("parts", "gx", "gy")),
        check_vma=False,
    )
```
